32 devices in a mesh: dp: 2 (over core), row: 4 (over y, x), col: 4 (over z).
Axes of the slice: x: 2, y: 2, z: 4, core: 2. Of those that a mesh axis runs over, the one named last changes fastest.
Arguments:
- images: bfloat16 [16, 4, 32, 2816], P('row', 'dp', None, 'col'), may hold values from -5 to 6.25
- cotangent: bfloat16 [16, 4, 32, 2816], P('row', 'dp', None, 'col'), may hold values from -6 to 6
- kernel: float32 [7, 7, 2816], P(None, None, 'col'), may hold values from -0.4 to 0.45
- w_in: bfloat16 [2816, 11264], P('col', ('row', 'dp')), may hold values from -0.109375 to 0.109375
- b_in: float32 [11264], P('row'), may hold values from -2.5 to 3
- grn_gamma: float32 [11264], P('row'), may hold values from -4 to 4
- grn_beta: float32 [11264], P('row'), may hold values from -3 to 3
- w_out: bfloat16 [11264, 2816], P(('row', 'dp'), 'col'), may hold values from -0.0546875 to 0.0546875
Outputs:
- result: bfloat16 [16, 4, 32, 2816], P('row', 'dp', None, 'col')
- x_grad: bfloat16 [16, 4, 32, 2816], P('row', 'dp', None, 'col')
- w_in_grad: float32 [2816, 11264], P('col', ('row', 'dp'))
- w_out_grad: float32 [11264, 2816], P(('row', 'dp'), 'col')
- kernel_grad: float32 [7, 7, 2816], P(None, None, 'col')
The draws below stay inside these ranges and needn't reach their ends.
All inputs are finite; a program needn't handle non-finite values.
Results may differ from the reference program's by a relative error of at most 0.018.
Values may be sent and summed in bfloat16 or wider, within the bound.
No kernel may reach another device: no remote copies, remote signals or barrier semaphores. Data moves between devices by JAX's collectives and lax.ppermute only.
A program may use at most 128 MiB of HBM per device.

```python
import jax
import jax.numpy as jnp
from jax import lax

C = 2816
FF = 11264
KSIZE = 7
BATCH = 2
WIDTH_PX = 32
H = 16
IMAGES = 4
CBLK = 704
ALLPIX = 2048
N_DP = 2
N_COL = 4


def draw_b_in(key, part):
    key = jax.random.fold_in(key, 5)
    position = jnp.arange(FF, dtype=jnp.float32) / (FF - 1)
    offset = -1.0 + 2.5 * position
    rough = jnp.clip(0.5 * jax.random.normal(key, (FF,), jnp.float32), -1.5, 1.5)
    return (offset + rough).astype(jnp.float32)


def draw_images(key, part):
    key = jax.random.fold_in(key, 11)
    position = jnp.arange(C, dtype=jnp.float32) / (C - 1)
    shape_all = (H, IMAGES, WIDTH_PX, C)
    offset = 0.3 + 0.9 * position
    rough = jnp.clip(jax.random.normal(key, shape_all, jnp.float32), -5.0, 5.0)
    return (rough + offset).astype(jnp.bfloat16)


def draw_kernel(key, part):
    key = jax.random.fold_in(key, 17)
    shape_all = (KSIZE, KSIZE, C)
    base = 1.0 / (KSIZE * KSIZE)
    rough = jnp.clip(0.1 * jax.random.normal(key, shape_all, jnp.float32), -0.4, 0.4)
    return (rough + base).astype(jnp.float32)


def steps_of(rng, extent, split, least, largest):
    loudness, own = 1.0, jax.random.fold_in(rng, 6)
    for dim, parts in split:
        heights = jnp.exp(jax.random.uniform(jax.random.fold_in(own, dim), (parts,), jnp.float32, least / len(split), largest / len(split)))
        loudness = loudness * jnp.repeat(heights, extent[dim] // parts).reshape([-1 if axis == dim else 1 for axis in range(len(extent))])
    return loudness


def gaussian(stream_key, dims, scale, limit, pieces=(), kind=jnp.bfloat16):
    gain = steps_of(stream_key, dims, pieces, -0.22, 0.18) if pieces else 1.0
    array = jax.random.normal(stream_key, dims, jnp.float32) * scale * gain
    return jnp.minimum(jnp.maximum(array, -limit), limit).astype(kind)


def setup_inputs(seed: int = 0) -> dict:
    keys = jax.random.split(jax.random.key(seed), 9)
    return {
        "images": draw_images(jax.random.fold_in(keys[8], 71), 0),
        "cotangent": gaussian(keys[1], (H, IMAGES, WIDTH_PX, C), 1.0, 6.0, ((0, 4), (1, 2), (3, 4))),
        "kernel": draw_kernel(jax.random.fold_in(keys[8], 71), 0),
        "w_in": gaussian(keys[3], (C, FF), C ** -0.5, 0.109375, ((0, 4), (1, 8))),
        "b_in": draw_b_in(jax.random.fold_in(keys[8], 71), 0),
        "grn_gamma": gaussian(keys[5], (FF,), 1.0, 4.0, ((0, 4),), jnp.float32),
        "grn_beta": gaussian(keys[6], (FF,), 0.5, 3.0, ((0, 4),), jnp.float32),
        "w_out": gaussian(keys[7], (FF, C), FF ** -0.5, 0.0546875, ((0, 8), (1, 4))),
    }


epsilon = 1e-06
root_half = 0.7071067811865476
inv_root_tau = 0.3989422804014327

def depthwise(padded, kernel, height, width):
    span = kernel.shape[0]
    result = jnp.zeros((height, padded.shape[1], width, padded.shape[3]), jnp.float32)
    for row_off in range(span):
        for col_off in range(span):
            window = padded[row_off:row_off + height, :, col_off:col_off + width, :]
            result = result + kernel[row_off, col_off] * window
    return result

def gelu_slope(hidden_pre):
    cumul = 0.5 * (1.0 + lax.erf(hidden_pre * root_half))
    return cumul + hidden_pre * jnp.exp(-0.5 * hidden_pre * hidden_pre) * inv_root_tau

def reference(images, cotangent, kernel, w_in, b_in, grn_gamma, grn_beta, w_out):
    reach = KSIZE // 2
    groups_x = images.reshape(H, N_DP, BATCH, WIDTH_PX, C).transpose(1, 0, 2, 3, 4)
    groups_c = cotangent.reshape(H, N_DP, BATCH, WIDTH_PX, C).transpose(1, 0, 2, 3, 4)

    def one_group(operands):
        tile_x, cot_tile = operands
        pad_spec = ((reach, reach), (0, 0), (reach, reach), (0, 0))
        padded_x = jnp.pad(tile_x.astype(jnp.float32), pad_spec)
        conv_out = depthwise(padded_x, kernel, H, WIDTH_PX)
        mean_pix = lax.optimization_barrier(jnp.mean(conv_out, axis=-1, keepdims=True))
        centred = conv_out - mean_pix
        var_pix = lax.optimization_barrier(jnp.mean(centred * centred, axis=-1, keepdims=True))
        inv_std = lax.rsqrt(var_pix + epsilon)
        standard = centred * inv_std
        normed = standard.astype(jnp.bfloat16).reshape(-1, C)
        hidden_sum = jnp.zeros((normed.shape[0], FF), jnp.float32)
        for block_idx in range(N_COL):
            lower = block_idx * CBLK
            piece = jnp.dot(normed[:, lower:lower + CBLK], w_in[lower:lower + CBLK, :], preferred_element_type=jnp.float32).astype(jnp.bfloat16)
            piece = lax.optimization_barrier(piece)
            hidden_sum = hidden_sum + piece.astype(jnp.float32)
        hidden_pre = hidden_sum + b_in
        hidden_act = jax.nn.gelu(hidden_pre, approximate=False)
        act_four = hidden_act.reshape(H, BATCH, WIDTH_PX, FF)
        norm_chan = jnp.sqrt(lax.optimization_barrier(jnp.sum(act_four * act_four, axis=(0, 2))) + epsilon)
        denom = lax.optimization_barrier(jnp.mean(norm_chan, axis=-1, keepdims=True)) + epsilon
        ratio_chan = norm_chan / denom
        gated = (grn_gamma * act_four * ratio_chan[None, :, None, :] + grn_beta + act_four).astype(jnp.bfloat16)
        gated_flat = gated.reshape(-1, FF)
        branch = jnp.dot(gated_flat, w_out, preferred_element_type=jnp.float32)
        result = (tile_x.astype(jnp.float32) + branch.reshape(tile_x.shape)).astype(jnp.bfloat16)
        cot_flat = cot_tile.reshape(-1, C)
        grad_flat = jnp.zeros((cot_flat.shape[0], FF), jnp.float32)
        for block_idx in range(N_COL):
            lower = block_idx * CBLK
            piece = jnp.dot(cot_flat[:, lower:lower + CBLK], w_out[:, lower:lower + CBLK].T, preferred_element_type=jnp.float32).astype(jnp.bfloat16)
            piece = lax.optimization_barrier(piece)
            grad_flat = grad_flat + piece.astype(jnp.float32)
        grad_gated = grad_flat.reshape(act_four.shape)
        pull_chan = lax.optimization_barrier(jnp.sum(grad_gated * grn_gamma * act_four, axis=(0, 2)))
        grad_norm = pull_chan / denom
        grad_act = grad_gated * (grn_gamma * ratio_chan[None, :, None, :] + 1.0) + act_four * (grad_norm / norm_chan)[None, :, None, :]
        grad_pre = (grad_act.reshape(-1, FF) * gelu_slope(hidden_pre)).astype(jnp.bfloat16)
        grad_normed = jnp.dot(grad_pre, w_in.T, preferred_element_type=jnp.float32).reshape(conv_out.shape)
        grad_w_out = jnp.dot(gated_flat.T, cot_flat, preferred_element_type=jnp.float32).astype(jnp.bfloat16)
        grad_w_in = jnp.dot(normed.T, grad_pre, preferred_element_type=jnp.float32).astype(jnp.bfloat16)
        first_back = lax.optimization_barrier(jnp.mean(grad_normed, axis=-1, keepdims=True))
        second_back = lax.optimization_barrier(jnp.mean(grad_normed * standard, axis=-1, keepdims=True))
        grad_conv = inv_std * (grad_normed - first_back - standard * second_back)
        padded_c = jnp.pad(grad_conv, pad_spec)
        spread = depthwise(padded_c, kernel[::-1, ::-1], H, WIDTH_PX)
        x_grad = (cot_tile.astype(jnp.float32) + spread).astype(jnp.bfloat16)
        kern_terms = []
        for row_off in range(KSIZE):
            for col_off in range(KSIZE):
                window = padded_x[row_off:row_off + H, :, col_off:col_off + WIDTH_PX, :]
                kern_terms.append(lax.optimization_barrier(jnp.sum(grad_conv * window, axis=(0, 1, 2))))
        kern_local = jnp.stack(kern_terms).reshape(KSIZE, KSIZE, C)
        return (result, x_grad, grad_w_in, grad_w_out, kern_local)
    results, x_grads, grads_in, grads_out, kern_parts = lax.map(one_group, (groups_x, groups_c))
    grads_in, grads_out = lax.optimization_barrier((grads_in, grads_out))
    scale_grad = 1.0 / jnp.sqrt(jnp.float32(ALLPIX))
    result = results.transpose(1, 0, 2, 3, 4).reshape(H, IMAGES, WIDTH_PX, C)
    x_grad = x_grads.transpose(1, 0, 2, 3, 4).reshape(H, IMAGES, WIDTH_PX, C)
    w_in_grad = lax.optimization_barrier(jnp.sum(grads_in.astype(jnp.float32), axis=0)) * scale_grad
    w_out_grad = lax.optimization_barrier(jnp.sum(grads_out.astype(jnp.float32), axis=0)) * scale_grad
    kernel_grad = lax.optimization_barrier(jnp.sum(kern_parts, axis=0)) * scale_grad
    return (result, x_grad, w_in_grad, w_out_grad, kernel_grad)
```

```python
import math

import jax
import jax.numpy as jnp
from jax import lax
from jax.sharding import PartitionSpec as P

epsilon = 1e-06
root_half = 0.7071067811865476
inv_root_tau = 0.3989422804014327
last_last = (((1,), (1,)), ((), ()))
first_first = (((0,), (0,)), ((), ()))
f32 = jnp.float32
bf16 = jnp.bfloat16


def swap(block, axis, bits):
    count = lax.axis_size(axis)
    return lax.ppermute(block, axis, [(i, i ^ bits) for i in range(count)])


def low_bit(m):
    return m & -m


def high_bit(m):
    return 1 << (m.bit_length() - 1)


def gather(block, axis, bit):
    held = [block]
    for m in range(1, lax.axis_size(axis)):
        step = bit(m)
        held.append(swap(held[m ^ step], axis, step))
    return held


def scatter_sum(parts, axis, bit):
    parts = list(parts)
    for m in range(lax.axis_size(axis) - 1, 0, -1):
        step = bit(m)
        got = swap(parts[m].astype(bf16), axis, step)
        parts[m ^ step] = parts[m ^ step].astype(f32) + got.astype(f32)
    return parts[0]


def gather_pixels(block):
    cols = gather(block, "col", low_bit)
    half = len(cols) // 2
    lower = gather(jnp.stack(cols[:half]), "row", low_bit)
    upper = gather(jnp.stack(cols[half:]), "row", high_bit)
    out = []
    for group in (lower, upper):
        for m in range(half):
            out.append(jnp.concatenate([piece[m] for piece in group], axis=0))
    return out


def scatter_pixels(blocks):
    half = len(blocks) // 2
    rows = lax.axis_size("row")
    done = []
    for group, bit in ((blocks[:half], low_bit), (blocks[half:], high_bit)):
        stacked = jnp.stack([b.reshape(rows, -1, b.shape[-1]) for b in group], axis=1)
        done.append(scatter_sum([stacked[q] for q in range(rows)], "row", bit))
    parts = [d[m].astype(bf16) for d in done for m in range(half)]
    return scatter_sum(parts, "col", low_bit)


def trade_pieces(pieces):
    return [pieces[0]] + [swap(pieces[m], "col", m) for m in range(1, len(pieces))]


def whole_weights(rows):
    count = lax.axis_size("col")
    share = rows.shape[0] // count
    me = lax.axis_index("col")
    pieces = [lax.dynamic_slice_in_dim(rows, (me ^ m) * share, share, axis=0) for m in range(count)]
    mine = jnp.stack(trade_pieces(pieces))
    other = swap(mine, "dp", 1)
    both = jnp.concatenate([mine, other], axis=1)
    return [both[m] for m in range(count)]


def whole_grads(blocks):
    count = len(blocks)
    share = blocks[0].shape[0] // 2
    me = lax.axis_index("col")
    stacked = jnp.stack(blocks)
    mine, other = stacked[:, :share], stacked[:, share:]
    got = swap(other, "dp", 1)
    total = (mine.astype(f32) + got.astype(f32)).astype(bf16)
    pieces = jnp.stack(trade_pieces([total[m] for m in range(count)]))
    return jnp.concatenate(
        [lax.dynamic_index_in_dim(pieces, me ^ j, 0, keepdims=False) for j in range(count)], axis=0
    )


def own_units(vector):
    count = lax.axis_size("col")
    span = vector.shape[0] // 2
    share = span // count
    me = lax.axis_index("col")
    side = lax.axis_index("dp")
    mine = lax.dynamic_slice_in_dim(vector, side * span + me * share, share)
    other = lax.dynamic_slice_in_dim(vector, (1 - side) * span + me * share, share)
    return jnp.concatenate([mine, other])


def add_over(value, axis):
    n = lax.axis_size(axis)
    step = 1
    while step < n:
        value = value + swap(value, axis, step)
        step *= 2
    return value


def extended(block, width):
    count = lax.axis_size("row")
    forward = [(i, i + 1) for i in range(count - 1)]
    backward = [(i + 1, i) for i in range(count - 1)]
    low = lax.ppermute(block[block.shape[0] - width :], "row", forward)
    high = lax.ppermute(block[:width], "row", backward)
    return jnp.concatenate([low, block, high], axis=0)


def depthwise(padded, kernel, height, width):
    span = kernel.shape[0]
    result = jnp.zeros((height, padded.shape[1], width, padded.shape[3]), f32)
    for row_off in range(span):
        for col_off in range(span):
            window = padded[row_off : row_off + height, :, col_off : col_off + width, :]
            result = result + kernel[row_off, col_off] * window
    return result


def pad_width(tile_in, reach):
    return jnp.pad(tile_in, ((0, 0), (0, 0), (reach, reach), (0, 0)))


def gelu_slope(hidden_pre):
    cumul = 0.5 * (1.0 + lax.erf(hidden_pre * root_half))
    return cumul + hidden_pre * jnp.exp(-0.5 * hidden_pre * hidden_pre) * inv_root_tau


def local(images, cotangent, kernel, w_in, b_in, grn_gamma, grn_beta, w_out):
    height, batch, width, chans = images.shape
    span = kernel.shape[0]
    reach = span // 2
    col_count = lax.axis_size("col")
    row_count = lax.axis_size("row")
    all_chans = chans * col_count
    all_units = b_in.shape[0] * row_count
    pixels = height * batch * width
    group_pix = pixels * row_count
    scale_grad = 1.0 / math.sqrt(group_pix * lax.axis_size("dp"))

    halo_x = extended(images, reach)
    w_in_all = whole_weights(w_in.T)
    cot_all = gather_pixels(cotangent.reshape(pixels, chans))
    w_out_all = whole_weights(w_out)
    bias, gamma, beta = own_units(b_in), own_units(grn_gamma), own_units(grn_beta)

    padded_x = pad_width(halo_x, reach).astype(f32)
    conv_out = depthwise(padded_x, kernel, height, width)
    mean_own = jnp.mean(conv_out, axis=-1)
    dev_own = conv_out - mean_own[..., None]
    stats = jnp.stack([mean_own, jnp.sum(dev_own * dev_own, axis=-1)])
    stats = [stats] + [swap(stats, "col", m) for m in range(1, col_count)]
    mean_pix = sum(s[0] for s in stats) / col_count
    var_pix = sum(s[1] + chans * (s[0] - mean_pix) ** 2 for s in stats) / all_chans
    inv_std = lax.rsqrt(var_pix + epsilon)[..., None]
    standard = (conv_out - mean_pix[..., None]) * inv_std
    normed_all = gather_pixels(standard.astype(bf16).reshape(pixels, chans))

    hidden_pre = bias + sum(
        lax.dot_general(x, w, last_last, preferred_element_type=f32)
        for x, w in zip(normed_all, w_in_all)
    )
    units = hidden_pre.shape[1]
    hidden_act = jax.nn.gelu(hidden_pre, approximate=False)
    act_four = hidden_act.reshape(-1, batch, width, units)
    norm_chan = jnp.sqrt(jnp.sum(act_four * act_four, axis=(0, 2)) + epsilon)
    norm_sum = add_over(add_over(jnp.sum(norm_chan, axis=-1), "row"), "col")
    denom = (norm_sum / all_units + epsilon)[:, None]
    ratio_chan = norm_chan / denom
    gated = (
        (gamma * act_four * ratio_chan[None, :, None, :] + beta + act_four)
        .astype(bf16)
        .reshape(group_pix, units)
    )
    branch = scatter_pixels(
        [jnp.dot(gated, w, preferred_element_type=f32).astype(bf16) for w in w_out_all]
    )
    result = (images.astype(f32) + branch.reshape(images.shape)).astype(bf16)

    grad_gated = sum(
        lax.dot_general(c, w, last_last, preferred_element_type=f32)
        for c, w in zip(cot_all, w_out_all)
    ).reshape(act_four.shape)
    pull_chan = jnp.sum(grad_gated * gamma * act_four, axis=(0, 2))
    grad_norm = pull_chan / denom
    grad_act = (
        grad_gated * (gamma * ratio_chan[None, :, None, :] + 1.0)
        + act_four * (grad_norm / norm_chan)[None, :, None, :]
    )
    grad_pre = (grad_act.reshape(group_pix, units) * gelu_slope(hidden_pre)).astype(bf16)
    grad_normed = scatter_pixels(
        [jnp.dot(grad_pre, w, preferred_element_type=f32).astype(bf16) for w in w_in_all]
    ).reshape(conv_out.shape)
    w_out_grad = (
        whole_grads(
            [
                lax.dot_general(gated, c, first_first, preferred_element_type=f32).astype(bf16)
                for c in cot_all
            ]
        ).astype(f32)
        * scale_grad
    )
    w_in_grad = (
        whole_grads(
            [
                lax.dot_general(grad_pre, x, first_first, preferred_element_type=f32).astype(bf16)
                for x in normed_all
            ]
        ).T.astype(f32)
        * scale_grad
    )

    sums = jnp.stack([jnp.sum(grad_normed, axis=-1), jnp.sum(grad_normed * standard, axis=-1)])
    sums = sum([swap(sums, "col", m) for m in range(1, col_count)], sums) / all_chans
    grad_conv = inv_std * (grad_normed - sums[0][..., None] - standard * sums[1][..., None])
    halo_cot = extended(grad_conv.astype(bf16), reach).astype(f32)
    spread = depthwise(pad_width(halo_cot, reach), kernel[::-1, ::-1], height, width)
    x_grad = (cotangent.astype(f32) + spread).astype(bf16)
    kern_terms = []
    for row_off in range(span):
        for col_off in range(span):
            window = padded_x[row_off : row_off + height, :, col_off : col_off + width, :]
            kern_terms.append(jnp.sum(grad_conv * window, axis=(0, 1, 2)))
    kern = jnp.stack(kern_terms).reshape(span, span, chans)
    for axis, step in (("dp", 1), ("row", 1), ("row", 2)):
        kern = kern.astype(bf16)
        kern = kern.astype(f32) + swap(kern, axis, step).astype(f32)
    kernel_grad = kern * scale_grad
    return (result, x_grad, w_in_grad, w_out_grad, kernel_grad)


def solution(mesh):
    return jax.shard_map(
        local,
        mesh=mesh,
        in_specs=(
            P("row", "dp", None, "col"),
            P("row", "dp", None, "col"),
            P(None, None, "col"),
            P("col", ("row", "dp")),
            P("row"),
            P("row"),
            P("row"),
            P(("row", "dp"), "col"),
        ),
        out_specs=(
            P("row", "dp", None, "col"),
            P("row", "dp", None, "col"),
            P("col", ("row", "dp")),
            P(("row", "dp"), "col"),
            P(None, None, "col"),
        ),
        check_vma=False,
    )
```

```python
import math

import jax
import jax.numpy as jnp
from jax import lax
from jax.experimental import pallas as pl
from jax.experimental.pallas import tpu as pltpu
from jax.sharding import PartitionSpec as P

epsilon = 1e-06
root_half = 0.7071067811865476
inv_root_tau = 0.3989422804014327
last_last = (((1,), (1,)), ((), ()))
first_first = (((0,), (0,)), ((), ()))
f32 = jnp.float32
bf16 = jnp.bfloat16


def swap(block, axis, bits):
    count = lax.axis_size(axis)
    return lax.ppermute(block, axis, [(i, i ^ bits) for i in range(count)])


def low_bit(m):
    return m & -m


def high_bit(m):
    return 1 << (m.bit_length() - 1)


def gather(block, axis, bit):
    held = [block]
    for m in range(1, lax.axis_size(axis)):
        step = bit(m)
        held.append(swap(held[m ^ step], axis, step))
    return held


def scatter_sum(parts, axis, bit):
    parts = list(parts)
    for m in range(lax.axis_size(axis) - 1, 0, -1):
        step = bit(m)
        got = swap(parts[m].astype(bf16), axis, step)
        parts[m ^ step] = parts[m ^ step].astype(f32) + got.astype(f32)
    return parts[0]


def gather_cols(block):
    cols = gather(block, "col", low_bit)
    half = len(cols) // 2
    return jnp.stack(cols[:half]), jnp.stack(cols[half:])


def gather_pixels(block):
    lower, upper = gather_cols(block)
    return gather(lower, "row", low_bit) + gather(upper, "row", high_bit)


def scatter_pixels(pieces):
    rows = lax.axis_size("row")
    done = [
        scatter_sum(pieces[:rows], "row", low_bit),
        scatter_sum(pieces[rows:], "row", high_bit),
    ]
    parts = [d[m].astype(bf16) for d in done for m in range(d.shape[0])]
    return scatter_sum(parts, "col", low_bit)


VMEM_BYTES = 44 * 2**20
in_vmem = pl.BlockSpec(memory_space=pltpu.VMEM)
in_smem = pl.BlockSpec(memory_space=pltpu.SMEM)


def call(body, outs, places, *operands, flops=0):
    moved = sum(math.prod(o.shape) * o.dtype.itemsize for o in list(operands) + list(outs))
    return pl.pallas_call(
        body,
        out_shape=outs,
        in_specs=[in_smem] + [in_vmem] * len(operands),
        out_specs=[in_vmem] * len(outs),
        compiler_params=pltpu.CompilerParams(vmem_limit_bytes=VMEM_BYTES),
        cost_estimate=pl.CostEstimate(flops=flops, bytes_accessed=moved, transcendentals=0),
    )(places, *operands)


def shape_of(dims, dtype):
    return jax.ShapeDtypeStruct(dims, dtype)


def piece_of(refs, places, rows, q, m):
    if len(refs) == 1:
        return refs[0][places[0] ^ q, m]
    half = refs[0].shape[0]
    return refs[q][m] if m < half else refs[rows + q][m - half]


def join_weights(places, mine, other):
    count, share, chans = mine.shape

    def body(places, mine, other, out):
        for m in range(count):
            out[m, :share, :] = mine[places[1] ^ m]
            out[m, share:, :] = other[places[1] ^ m]

    if share % 16:
        order = places[1] ^ jnp.arange(count)
        return jnp.concatenate([mine[order], other[order]], axis=1)
    return call(body, [shape_of((count, 2 * share, chans), bf16)], places, mine, other)[0]


def whole_weights(rows, places):
    count = lax.axis_size("col")
    mine = lax.all_to_all(rows.reshape(count, -1, rows.shape[1]), "col", 0, 0)
    return join_weights(places, mine, swap(mine, "dp", 1))


def hidden_kernel(places, pieces, weights, bias, dims):
    rows, height, batch, width = dims
    count, units, chans = weights.shape
    pixels = height * batch * width

    def body(places, *refs):
        xs = refs[: len(pieces)]
        w, b, act, slope, square = refs[len(pieces) :]
        total = jnp.zeros((batch, units), f32)
        for q in range(rows):
            pre = b[...]
            for m in range(count):
                pre = pre + lax.dot_general(
                    piece_of(xs, places, rows, q, m), w[m], last_last, preferred_element_type=f32
                )
            cumul = 0.5 * (1.0 + lax.erf(pre * root_half))
            value = pre * cumul
            act[q * pixels : (q + 1) * pixels, :] = value
            slope[q * pixels : (q + 1) * pixels, :] = cumul + pre * jnp.exp(-0.5 * pre * pre) * inv_root_tau
            total = total + jnp.sum((value * value).reshape(height, batch, width, units), axis=(0, 2))
        square[...] = total

    full = (rows * pixels, units)
    return call(
        body,
        [shape_of(full, f32), shape_of(full, f32), shape_of((batch, units), f32)],
        places,
        *pieces,
        weights,
        bias[None],
        flops=2 * rows * pixels * units * chans * count,
    )


def back_kernel(places, pieces, weights, act, dims):
    rows, height, batch, width = dims
    count, units, chans = weights.shape
    pixels = height * batch * width

    def body(places, *refs):
        xs = refs[: len(pieces)]
        w, act, grad, pull = refs[len(pieces) :]
        total = jnp.zeros((batch, units), f32)
        for q in range(rows):
            value = jnp.zeros((pixels, units), f32)
            for m in range(count):
                value = value + lax.dot_general(
                    piece_of(xs, places, rows, q, m), w[m], last_last, preferred_element_type=f32
                )
            grad[q * pixels : (q + 1) * pixels, :] = value
            both = value * act[q * pixels : (q + 1) * pixels, :]
            total = total + jnp.sum(both.reshape(height, batch, width, units), axis=(0, 2))
        pull[...] = total

    return call(
        body,
        [shape_of(act.shape, f32), shape_of((batch, units), f32)],
        places,
        *pieces,
        weights,
        act,
        flops=2 * rows * pixels * units * chans * count,
    )


def project_kernel(places, rows_of, operands, weights, dims, together):
    rows, height, batch, width = dims
    count, units, chans = weights.shape
    pixels = height * batch * width
    half = count // 2

    def body(places, *refs):
        ins = refs[: len(operands)]
        w, kept = refs[len(operands) : len(operands) + 2]
        outs = refs[len(operands) + 2 :]

        def spread(vector):
            wide = jnp.broadcast_to(vector[None, :, None, :], (height, batch, width, units))
            return wide.reshape(pixels, units)

        for q in range(rows):
            part = slice(q * pixels, (q + 1) * pixels)
            blocks = [r[part, :] if r.shape[0] == rows * pixels else r[...] for r in ins]
            made = rows_of(blocks, spread).astype(bf16)
            kept[part, :] = made
            for m in range(count):
                value = jnp.dot(made, w[m], preferred_element_type=f32).astype(bf16)
                if together:
                    outs[0][places[0] ^ q, m] = value
                elif m < half:
                    outs[q][m] = value
                else:
                    outs[rows + q][m - half] = value

    if together:
        outs = [shape_of((rows, count, pixels, chans), bf16)]
    else:
        outs = [shape_of((half, pixels, chans), bf16)] * (2 * rows)
    got = call(
        body,
        [shape_of((rows * pixels, units), bf16)] + outs,
        places,
        *operands,
        weights,
        flops=2 * rows * pixels * units * chans * count,
    )
    return got[0], got[1:]


def grads_kernel(places, left, pieces, dims, count, chans):
    rows, height, batch, width = dims
    units = left.shape[1]
    share = units // 2

    def body(places, left, *refs):
        xs = refs[: len(pieces)]
        mine, other = refs[len(pieces) :]
        turned = left[...].T
        for m in range(count):
            x = jnp.concatenate([piece_of(xs, places, rows, q, m) for q in range(rows)], axis=0)
            value = jnp.dot(turned, x, preferred_element_type=f32)
            mine[places[1] ^ m] = value[:share].astype(bf16)
            other[places[1] ^ m] = value[share:].astype(bf16)

    return call(
        body,
        [shape_of((count, share, chans), bf16)] * 2,
        places,
        left,
        *pieces,
        flops=2 * left.shape[0] * units * chans * count,
    )


def whole_grads(mine, other):
    total = (mine.astype(f32) + swap(other, "dp", 1).astype(f32)).astype(bf16)
    return lax.all_to_all(total, "col", 0, 0).reshape(-1, mine.shape[-1])


def own_units(vector):
    count = lax.axis_size("col")
    span = vector.shape[0] // 2
    share = span // count
    me = lax.axis_index("col")
    side = lax.axis_index("dp")
    mine = lax.dynamic_slice_in_dim(vector, side * span + me * share, share)
    other = lax.dynamic_slice_in_dim(vector, (1 - side) * span + me * share, share)
    return jnp.concatenate([mine, other])


def add_over(value, axis):
    n = lax.axis_size(axis)
    step = 1
    while step < n:
        value = value + swap(value, axis, step)
        step *= 2
    return value


def extended(block, width):
    count = lax.axis_size("row")
    forward = [(i, i + 1) for i in range(count - 1)]
    backward = [(i + 1, i) for i in range(count - 1)]
    low = lax.ppermute(block[block.shape[0] - width :], "row", forward)
    high = lax.ppermute(block[:width], "row", backward)
    return jnp.concatenate([low, block, high], axis=0)


def depthwise(padded, kernel, height, width):
    span = kernel.shape[0]
    result = jnp.zeros((height, padded.shape[1], width, padded.shape[3]), f32)
    for row_off in range(span):
        for col_off in range(span):
            window = padded[row_off : row_off + height, :, col_off : col_off + width, :]
            result = result + kernel[row_off, col_off] * window
    return result


def pad_width(tile_in, reach):
    return jnp.pad(tile_in, ((0, 0), (0, 0), (reach, reach), (0, 0)))


def local(images, cotangent, kernel, w_in, b_in, grn_gamma, grn_beta, w_out):
    height, batch, width, chans = images.shape
    span = kernel.shape[0]
    reach = span // 2
    col_count = lax.axis_size("col")
    row_count = lax.axis_size("row")
    all_chans = chans * col_count
    all_units = b_in.shape[0] * row_count
    pixels = height * batch * width
    group_pix = pixels * row_count
    scale_grad = 1.0 / math.sqrt(group_pix * lax.axis_size("dp"))

    places = jnp.stack([lax.axis_index("row"), lax.axis_index("col")]).astype(jnp.int32)
    dims = (row_count, height, batch, width)

    halo_x = extended(images, reach)
    w_in_all = whole_weights(w_in.T, places)
    cot_cols = jnp.concatenate(gather_cols(cotangent.reshape(pixels, chans)))
    cot_all = [lax.all_gather(cot_cols, "row")]
    w_out_all = whole_weights(w_out, places)
    bias, gamma, beta = own_units(b_in), own_units(grn_gamma), own_units(grn_beta)

    padded_x = pad_width(halo_x, reach).astype(f32)
    conv_out = depthwise(padded_x, kernel, height, width)
    mean_own = jnp.mean(conv_out, axis=-1)
    dev_own = conv_out - mean_own[..., None]
    stats = jnp.stack([mean_own, jnp.sum(dev_own * dev_own, axis=-1)])
    stats = [stats] + [swap(stats, "col", m) for m in range(1, col_count)]
    mean_pix = sum(s[0] for s in stats) / col_count
    var_pix = sum(s[1] + chans * (s[0] - mean_pix) ** 2 for s in stats) / all_chans
    inv_std = lax.rsqrt(var_pix + epsilon)[..., None]
    standard = (conv_out - mean_pix[..., None]) * inv_std
    normed_all = gather_pixels(standard.astype(bf16).reshape(pixels, chans))

    act, slope, square = hidden_kernel(places, normed_all, w_in_all, bias, dims)
    norm_chan = jnp.sqrt(square + epsilon)
    norm_sum = add_over(add_over(jnp.sum(norm_chan, axis=-1), "row"), "col")
    denom = (norm_sum / all_units + epsilon)[:, None]
    gain = gamma * (norm_chan / denom) + 1.0
    grad_gated, pull = back_kernel(places, cot_all, w_out_all, act, dims)
    share_back = gamma * pull / denom / norm_chan

    grad_pre, grad_parts = project_kernel(
        places,
        lambda b, spread: (b[0] * spread(b[3]) + b[1] * spread(b[4])) * b[2],
        [grad_gated, act, slope, gain, share_back],
        w_in_all,
        dims,
        False,
    )
    gated, out_parts = project_kernel(
        places,
        lambda b, spread: b[0] * spread(b[1]) + b[2],
        [act, gain, beta[None]],
        w_out_all,
        dims,
        True,
    )
    w_in_mine, w_in_other = grads_kernel(places, grad_pre, normed_all, dims, col_count, chans)
    w_out_mine, w_out_other = grads_kernel(places, gated, cot_all, dims, col_count, chans)
    w_in_grad = whole_grads(w_in_mine, w_in_other).T.astype(f32) * scale_grad
    w_out_grad = whole_grads(w_out_mine, w_out_other).astype(f32) * scale_grad

    grad_normed = scatter_pixels(grad_parts).reshape(conv_out.shape)
    branch_rows = lax.psum_scatter(
        out_parts[0].reshape(-1, chans), "row", scatter_dimension=0, tiled=True
    ).reshape(col_count, pixels, chans)
    branch = scatter_sum([branch_rows[m] for m in range(col_count)], "col", low_bit)
    result = (images.astype(f32) + branch.reshape(images.shape).astype(f32)).astype(bf16)

    sums = jnp.stack([jnp.sum(grad_normed, axis=-1), jnp.sum(grad_normed * standard, axis=-1)])
    sums = sum([swap(sums, "col", m) for m in range(1, col_count)], sums) / all_chans
    grad_conv = inv_std * (grad_normed - sums[0][..., None] - standard * sums[1][..., None])
    halo_cot = extended(grad_conv.astype(bf16), reach).astype(f32)
    spread = depthwise(pad_width(halo_cot, reach), kernel[::-1, ::-1], height, width)
    x_grad = (cotangent.astype(f32) + spread).astype(bf16)
    kern_terms = []
    for row_off in range(span):
        for col_off in range(span):
            window = padded_x[row_off : row_off + height, :, col_off : col_off + width, :]
            kern_terms.append(jnp.sum(grad_conv * window, axis=(0, 1, 2)))
    kern = jnp.stack(kern_terms).reshape(span, span, chans)
    steps = [("dp", 1)] + [("row", 1 << i) for i in range((row_count - 1).bit_length())]
    for axis, step in steps:
        kern = kern.astype(bf16)
        kern = kern.astype(f32) + swap(kern, axis, step).astype(f32)
    kernel_grad = kern * scale_grad
    return (result, x_grad, w_in_grad, w_out_grad, kernel_grad)


def solution(mesh):
    return jax.shard_map(
        local,
        mesh=mesh,
        in_specs=(
            P("row", "dp", None, "col"),
            P("row", "dp", None, "col"),
            P(None, None, "col"),
            P("col", ("row", "dp")),
            P("row"),
            P("row"),
            P("row"),
            P(("row", "dp"), "col"),
        ),
        out_specs=(
            P("row", "dp", None, "col"),
            P("row", "dp", None, "col"),
            P("col", ("row", "dp")),
            P(("row", "dp"), "col"),
            P(None, None, "col"),
        ),
        check_vma=False,
    )
```

```python
import math

import jax
import jax.numpy as jnp
from jax import lax
from jax.experimental import pallas as pl
from jax.experimental.layout import Layout, with_layout_constraint
from jax.experimental.pallas import tpu as pltpu
from jax.sharding import PartitionSpec as P

epsilon = 1e-06
root_half = 0.7071067811865476
inv_root_tau = 0.3989422804014327
last_last = (((1,), (1,)), ((), ()))
f32 = jnp.float32
bf16 = jnp.bfloat16


def swap(block, axis, bits):
    count = lax.axis_size(axis)
    return lax.ppermute(block, axis, [(i, i ^ bits) for i in range(count)])


def pin(block):
    return with_layout_constraint(block, Layout(tuple(range(block.ndim))))


def after(blocks, *earlier):
    kept, _ = lax.optimization_barrier((blocks, earlier))
    return kept


def first_hops(block, every=False):
    count = lax.axis_size("col")
    bits = range(1, count) if every else [1 << i for i in range((count - 1).bit_length())]
    return {bit: pin(swap(block, "col", bit)) for bit in bits}


def gather_cols(block, hops):
    held = {0: pin(block)} | hops
    count = lax.axis_size("col")
    for m in sorted(range(1, count), key=lambda m: m.bit_count()):
        if m not in held:
            held[m] = pin(swap(held[m & (m - 1)], "col", m & -m))
    return [held[m] for m in range(count)]


def stack_cols(blocks):
    return [pin(jnp.stack([blocks[m] for m in side])) for side in col_order(len(blocks))]


def gather_rows(block, bits):
    held = {0: block}
    for bit in bits:
        held.update({q ^ bit: pin(swap(held[q], "row", bit)) for q in list(held)})
    return [held[q] for q in range(lax.axis_size("row"))]


def row_bits():
    return [1 << i for i in range((lax.axis_size("row") - 1).bit_length())]


def col_order(count):
    held, step = [0], count // 2
    while step > 1:
        held = held + [m ^ step for m in held]
        step //= 2
    return held, [m ^ 1 for m in held]


def halve_sum(near, far, axis, bits, earlier=()):
    for place, bit in enumerate(bits):
        got = swap(pin(far.astype(bf16)), axis, bit)
        if earlier:
            got = after(got, *earlier)
        total = near.astype(f32) + got.astype(f32)
        half = total.shape[0] // 2
        near, far = total[:half], total[half:]
    return total[0]


VMEM_BYTES = 44 * 2**20
in_vmem = pl.BlockSpec(memory_space=pltpu.VMEM)
in_smem = pl.BlockSpec(memory_space=pltpu.SMEM)


def call(body, outs, places, *operands):
    return pl.pallas_call(
        body,
        out_shape=outs,
        in_specs=[in_smem] + [in_vmem] * len(operands),
        out_specs=[in_vmem] * len(outs),
        compiler_params=pltpu.CompilerParams(vmem_limit_bytes=VMEM_BYTES),
        cost_estimate=pl.CostEstimate(flops=0, bytes_accessed=0, transcendentals=0),
    )(places, *operands)


def shape_of(dims, dtype):
    return jax.ShapeDtypeStruct(dims, dtype)


def piece_of(refs, places, rows, q, m):
    half = refs[-1].shape[-3] if len(refs) > 1 else refs[0].shape[1] // 2
    side, place = m // half, m % half
    if len(refs) == 1:
        return refs[0][places[0] ^ q, m]
    return refs[side * rows + q][place]


def cut_units(w, out, count):
    share = w.shape[1] // count
    for j in range(count):
        out[j] = w[:, j * share : (j + 1) * share]


def prepare(places, images, cotangent, w_in, reach):
    height, batch, width, chans = cotangent.shape
    count = lax.axis_size("col")
    span = height * width

    def body(places, images, cot, w_in, pieces, turned, low, high):
        cut_units(w_in, pieces, count)
        for b in range(batch):
            turned[:, b * span : (b + 1) * span] = cot[:, b].reshape(span, chans).T
        low[...] = images[height - reach :]
        high[...] = images[:reach]

    edge = shape_of((reach, batch, width, chans), bf16)
    outs = [
        shape_of((count, chans, w_in.shape[1] // count), bf16),
        shape_of((chans, batch * span), bf16),
        edge,
        edge,
    ]
    return call(body, outs, places, images, cotangent, w_in)


def prepare_out(places, w_out_turned):
    count = lax.axis_size("col")
    chans, units = w_out_turned.shape

    def body(places, w, pieces):
        cut_units(w, pieces, count)

    return call(body, [shape_of((count, chans, units // count), bf16)], places, w_out_turned)[0]


def join_weights(places, mine, other):
    count, chans, share = mine.shape
    units = 2 * share
    order = sum(col_order(count), [])

    def body(places, mine, other, out, turned):
        for place, m in enumerate(order):
            j = places[1] ^ m
            both = jnp.concatenate([mine[j], other[j]], axis=1)
            turned[place] = both
            out[place] = both.T

    outs = [shape_of((count, units, chans), bf16), shape_of((count, chans, units), bf16)]
    return call(body, outs, places, mine, other)


def image_sums(value, batch):
    span = value.shape[1] // batch
    return [jnp.sum(value[:, b * span : (b + 1) * span], axis=1, keepdims=True) for b in range(batch)]


def hidden_kernel(places, pieces, weights, bias, dims):
    rows, batch, pixels = dims
    count, units, chans = weights.shape

    def body(places, *refs):
        xs = refs[: len(pieces)]
        w, b, act, slope, square = refs[len(pieces) :]
        total = jnp.zeros((units, batch), f32)
        for q in range(rows):
            pre = b[...]
            for m in range(count):
                pre = pre + jnp.dot(w[m], piece_of(xs, places, rows, q, m), preferred_element_type=f32)
            cumul = 0.5 * (1.0 + lax.erf(pre * root_half))
            value = pre * cumul
            part = slice(q * pixels, (q + 1) * pixels)
            act[:, part] = value
            slope[:, part] = cumul + pre * jnp.exp(-0.5 * pre * pre) * inv_root_tau
            total = total + jnp.concatenate(image_sums(value * value, batch), axis=1)
        square[...] = total

    full = (units, rows * pixels)
    return call(
        body,
        [shape_of(full, f32), shape_of(full, f32), shape_of((units, batch), f32)],
        places,
        *pieces,
        weights,
        bias[:, None],
    )


def back_kernel(places, pieces, weights, act, dims):
    rows, batch, pixels = dims
    count, units, chans = weights.shape

    def body(places, *refs):
        xs = refs[: len(pieces)]
        w, act, grad, pull = refs[len(pieces) :]
        total = jnp.zeros((units, batch), f32)
        for q in range(rows):
            value = jnp.zeros((units, pixels), f32)
            for m in range(count):
                value = value + jnp.dot(
                    w[m], piece_of(xs, places, rows, q, m), preferred_element_type=f32
                )
            part = slice(q * pixels, (q + 1) * pixels)
            grad[:, part] = value
            total = total + jnp.concatenate(image_sums(value * act[:, part], batch), axis=1)
        pull[...] = total

    return call(
        body,
        [shape_of(act.shape, f32), shape_of((units, batch), f32)],
        places,
        *pieces,
        weights,
        act,
    )


def project_kernel(places, made_of, operands, turned, dims, splits):
    rows, batch, pixels = dims
    count, chans, units = turned.shape
    half = count // 2

    def body(places, *refs):
        ins = refs[: len(operands)]
        w, kept = refs[len(operands) : len(operands) + 2]
        outs = refs[len(operands) + 2 :]

        def spread(vectors):
            span = (units, pixels // batch)
            return jnp.concatenate(
                [jnp.broadcast_to(vectors[:, b : b + 1], span) for b in range(batch)], axis=1
            )

        for q in range(rows):
            part = slice(q * pixels, (q + 1) * pixels)
            blocks = [r[:, part] if r.shape[1] == rows * pixels else r[...] for r in ins]
            made = made_of(blocks, spread).astype(bf16)
            kept[:, part] = made
            for m in range(count):
                value = jnp.dot(w[m], made, preferred_element_type=f32).astype(bf16)
                if not splits:
                    outs[0][places[0] ^ q, m] = value
                else:
                    side, place = m // half, m % half
                    bit = splits[side]
                    kind = 1 if q & bit else 0
                    outs[2 * side + kind][queue[side].index(q & ~bit), place] = value

    queue = [sorted({q & ~bit for q in range(rows)}) for bit in splits or []]
    if not splits:
        outs = [shape_of((rows, count, chans, pixels), bf16)]
    else:
        outs = [shape_of((rows // 2, half, chans, pixels), bf16)] * 4
    got = call(
        body, [shape_of((units, rows * pixels), bf16)] + outs, places, *operands, turned
    )
    return got[0], got[1:]


def grads_kernel(places, left, pieces, dims, count, chans):
    rows, batch, pixels = dims
    units = left.shape[0]
    share = units // 2
    order = sum(col_order(count), [])

    def body(places, left, *refs):
        xs = refs[: len(pieces)]
        mine, other = refs[len(pieces) :]
        for place, m in enumerate(order):
            x = jnp.concatenate([piece_of(xs, places, rows, q, place) for q in range(rows)], axis=1)
            value = lax.dot_general(x, left[...], last_last, preferred_element_type=f32).astype(bf16)
            mine[places[1] ^ m] = value[:, :share]
            other[places[1] ^ m] = value[:, share:]

    return call(body, [shape_of((count, chans, share), bf16)] * 2, places, left, *pieces)


def add_kernel(places, mine, got):
    def body(places, mine, got, out):
        for j in range(mine.shape[0]):
            out[j] = (mine[j].astype(f32) + got[j].astype(f32)).astype(bf16)

    return call(body, [shape_of(mine.shape, bf16)], places, mine, got)[0]


def finish_kernel(places, pieces, scale):
    count, chans, share = pieces.shape

    def body(places, pieces, out):
        wide = jnp.concatenate([pieces[j].astype(f32) for j in range(count)], axis=1)
        out[...] = wide * scale

    return call(body, [shape_of((chans, count * share), f32)], places, pieces)[0]


def own_units(vector):
    count = lax.axis_size("col")
    span = vector.shape[0] // 2
    share = span // count
    me = lax.axis_index("col")
    side = lax.axis_index("dp")
    mine = lax.dynamic_slice_in_dim(vector, side * span + me * share, share)
    other = lax.dynamic_slice_in_dim(vector, (1 - side) * span + me * share, share)
    return jnp.concatenate([mine, other])


def add_over(value, axis):
    n = lax.axis_size(axis)
    step = 1
    while step < n:
        value = value + swap(value, axis, step)
        step *= 2
    return value


def exchange_rows(low, high):
    count = lax.axis_size("row")
    forward = [(i, i + 1) for i in range(count - 1)]
    backward = [(i + 1, i) for i in range(count - 1)]
    return lax.ppermute(low, "row", forward), lax.ppermute(high, "row", backward)


EDGE = 8


def fill_padded(padded, low, mid, high):
    reach, height, width = low.shape[0], mid.shape[0], mid.shape[2]
    zeros = jnp.zeros(padded.shape[:2] + (EDGE, padded.shape[3]), f32)
    padded[:, :, :EDGE, :] = zeros
    padded[:, :, EDGE + width :, :] = zeros
    padded[:reach, :, EDGE : EDGE + width, :] = low[...].astype(f32)
    padded[reach : reach + height, :, EDGE : EDGE + width, :] = mid[...].astype(f32)
    padded[reach + height :, :, EDGE : EDGE + width, :] = high[...].astype(f32)


def lane_chunks(chans):
    return [slice(c, min(c + 128, chans)) for c in range(0, chans, 128)]


def depthwise(places, low, mid, high, kernel, extra, flip):
    height, batch, width, chans = mid.shape
    span = kernel.shape[0]
    reach = span // 2

    def body(places, low, mid, high, kern, *refs):
        out, padded = refs[-2:]
        fill_padded(padded, low, mid, high)

        @pl.loop(0, batch)
        def _(b):
            for lanes in lane_chunks(chans):
                sums = [None] * height
                for r in range(height + 2 * reach):
                    for j in range(span):
                        start = EDGE + j - reach
                        window = padded[r, b, start : start + width, lanes]
                        for h in range(max(0, r - span + 1), min(height, r + 1)):
                            i = r - h
                            tap = (span - 1 - i, span - 1 - j) if flip else (i, j)
                            term = kern[tap[0], tap[1] : tap[1] + 1, lanes] * window
                            sums[h] = term if sums[h] is None else sums[h] + term
                for h in range(height):
                    value = sums[h]
                    if extra is not None:
                        value = value + refs[0][h, b, :, lanes].astype(f32)
                    out[h, b, :, lanes] = value.astype(out.dtype)

    more = [] if extra is None else [extra]
    operands = [low, mid, high, kernel] + more
    return pl.pallas_call(
        body,
        out_shape=shape_of(mid.shape, f32 if extra is None else bf16),
        in_specs=[in_smem] + [in_vmem] * len(operands),
        out_specs=in_vmem,
        scratch_shapes=[pltpu.VMEM((height + 2 * reach, batch, width + 2 * EDGE, chans), f32)],
        compiler_params=pltpu.CompilerParams(vmem_limit_bytes=VMEM_BYTES),
        cost_estimate=pl.CostEstimate(flops=0, bytes_accessed=0, transcendentals=0),
    )(places, *operands)


def kernel_terms(places, low, mid, high, grad, span):
    height, batch, width, chans = mid.shape
    reach = span // 2

    def body(places, low, mid, high, grad, out, padded, sums):
        fill_padded(padded, low, mid, high)
        for lanes in lane_chunks(chans):
            for i in range(span):

                def step(b, total):
                    total = list(total)
                    for h in range(height):
                        piece = grad[h, b, :, lanes]
                        for j in range(span):
                            start = EDGE + j - reach
                            both = piece * padded[h + i, b, start : start + width, lanes]
                            total[j] = total[j] + jnp.sum(both.reshape(-1, 8, both.shape[1]), axis=0)
                    return tuple(total)

                zero = jnp.zeros((8, lanes.stop - lanes.start), f32)
                total = lax.fori_loop(0, batch, step, (zero,) * span)
                for j in range(span):
                    sums[i, j, :, lanes] = total[j]
        for i in range(span):
            out[i] = jnp.sum(sums[i], axis=1)

    operands = [low, mid, high, grad]
    return pl.pallas_call(
        body,
        out_shape=shape_of((span, span, chans), f32),
        in_specs=[in_smem] + [in_vmem] * len(operands),
        out_specs=in_vmem,
        scratch_shapes=[
            pltpu.VMEM((height + 2 * reach, batch, width + 2 * EDGE, chans), f32),
            pltpu.VMEM((span, span, 8, chans), f32),
        ],
        compiler_params=pltpu.CompilerParams(vmem_limit_bytes=VMEM_BYTES),
        cost_estimate=pl.CostEstimate(flops=0, bytes_accessed=0, transcendentals=0),
    )(places, *operands)


def local(images, cotangent, kernel, w_in, b_in, grn_gamma, grn_beta, w_out):
    height, batch, width, chans = images.shape
    span = kernel.shape[0]
    reach = span // 2
    col_count = lax.axis_size("col")
    row_count = lax.axis_size("row")
    all_chans = chans * col_count
    all_units = b_in.shape[0] * row_count
    pixels = height * batch * width
    group_pix = pixels * row_count
    scale_grad = 1.0 / math.sqrt(group_pix * lax.axis_size("dp"))

    places = jnp.stack([lax.axis_index("row"), lax.axis_index("col")]).astype(jnp.int32)
    dims = (row_count, batch, pixels)

    def turned(tile):
        return tile.transpose(3, 1, 0, 2).reshape(chans, pixels)

    def natural(block):
        return block.reshape(chans, batch, height, width).transpose(2, 1, 3, 0)


    pieces, cot_turned, low, high = prepare(places, images, cotangent, w_in, reach)
    cot_hops = first_hops(cot_turned, True)
    mine = lax.all_to_all(pieces, "col", 0, 0)
    w_in_all, w_in_turned = join_weights(places, mine, swap(mine, "dp", 1))
    w_in_there = mine
    low, high = exchange_rows(low, high)
    bias, gamma, beta = own_units(b_in), own_units(grn_gamma), own_units(grn_beta)

    conv_out = depthwise(places, low, images, high, kernel, None, False)
    mean_own = jnp.mean(conv_out, axis=-1)
    dev_own = conv_out - mean_own[..., None]
    stats = jnp.stack([mean_own, jnp.sum(dev_own * dev_own, axis=-1)])
    stats = after(stats, cot_hops)
    cot_cols = gather_cols(cot_turned, cot_hops)
    stats = [stats] + [swap(stats, "col", m) for m in range(1, col_count)]
    stats = after(stats, w_in_there)
    mean_pix = sum(s[0] for s in stats) / col_count
    var_pix = sum(s[1] + chans * (s[0] - mean_pix) ** 2 for s in stats) / all_chans
    inv_std = lax.rsqrt(var_pix + epsilon)[..., None]
    standard = (conv_out - mean_pix[..., None]) * inv_std
    bits = row_bits()
    normed = turned(standard.astype(bf16))
    normed_cols = gather_cols(normed, first_hops(normed))
    even, odd = stack_cols(normed_cols)
    normed_all = gather_rows(even, bits) + gather_rows(odd, bits[::-1])
    cot_all = [pin(lax.all_gather(pin(jnp.concatenate(stack_cols(cot_cols))), "row"))]
    pieces = after(prepare_out(places, w_out.T), normed_cols)
    w_out_there = lax.all_to_all(pieces, "col", 0, 0)
    act, slope, square = hidden_kernel(places, normed_all, w_in_all, bias, dims)
    w_out_there = after(w_out_there, normed_all)
    w_out_all, w_out_turned = join_weights(places, w_out_there, swap(w_out_there, "dp", 1))
    norm_chan = jnp.sqrt(square + epsilon)
    norm_sum = add_over(add_over(jnp.sum(norm_chan, axis=0), "row"), "col")
    denom = norm_sum / all_units + epsilon
    gamma, beta = gamma[:, None], beta[:, None]
    gain = gamma * (norm_chan / denom) + 1.0
    grad_gated, pull = back_kernel(places, cot_all, w_out_all, act, dims)
    share_back = gamma * pull / denom / norm_chan

    grad_pre, grad_parts = project_kernel(
        places,
        lambda b, spread: (b[0] * spread(b[3]) + b[1] * spread(b[4])) * b[2],
        [grad_gated, act, slope, gain, share_back],
        w_in_turned,
        dims,
        (bits[0], bits[-1]),
    )
    gated, out_parts = project_kernel(
        places,
        lambda b, spread: b[0] * spread(b[1]) + b[2],
        [act, gain, beta],
        w_out_turned,
        dims,
        (),
    )
    w_in_mine, w_in_other = grads_kernel(places, grad_pre, normed_all, dims, col_count, chans)
    w_out_mine, w_out_other = grads_kernel(places, gated, cot_all, dims, col_count, chans)
    w_out_sums = add_kernel(places, w_out_mine, swap(w_out_other, "dp", 1))
    w_out_back = lax.all_to_all(w_out_sums, "col", 0, 0)
    w_out_grad = finish_kernel(places, w_out_back, scale_grad).T
    w_in_sums = add_kernel(places, w_in_mine, swap(w_in_other, "dp", 1))

    near_a, far_a, near_b, far_b = grad_parts
    even = halve_sum(near_a, far_a, "row", bits, (w_in_other,))
    odd = halve_sum(near_b, far_b, "row", bits[::-1], (w_in_other,))
    down = [1 << i for i in range((col_count - 1).bit_length())]
    branch_rows = pin(
        lax.psum_scatter(
            pin(after(out_parts[0], even, odd).reshape(-1, pixels)), "row", scatter_dimension=0, tiled=True
        )
    ).reshape(col_count, chans, pixels)
    odd = after(odd, w_out_back)
    grad_normed = natural(pin(halve_sum(even, odd, "col", down)))

    sums = jnp.stack([jnp.sum(grad_normed, axis=-1), jnp.sum(grad_normed * standard, axis=-1)])
    sums = sum([swap(sums, "col", m) for m in range(1, col_count)], sums) / all_chans
    branch_rows = after(branch_rows, sums)
    w_in_sums = after(w_in_sums, sums)
    w_in_grad = finish_kernel(places, lax.all_to_all(w_in_sums, "col", 0, 0), scale_grad)
    grad_conv = inv_std * (grad_normed - sums[0][..., None] - standard * sums[1][..., None])
    edge = grad_conv.astype(bf16)
    low_grad, high_grad = exchange_rows(edge[height - reach :], edge[:reach])
    x_grad = depthwise(places, low_grad, grad_conv, high_grad, kernel, cotangent, True)
    kern = kernel_terms(places, low, images, high, after(grad_conv, low_grad, high_grad), span)
    steps = [("dp", 1)] + [("row", 1 << i) for i in range((row_count - 1).bit_length())]
    for axis, step in steps:
        kern = kern.astype(bf16)
        kern = kern.astype(f32) + swap(kern, axis, step).astype(f32)
    kernel_grad = kern * scale_grad
    branch = halve_sum(branch_rows[: col_count // 2], branch_rows[col_count // 2 :], "col", down, (x_grad, kern))
    branch = natural(pin(branch))
    result = (images.astype(f32) + branch.astype(f32)).astype(bf16)
    return (result, x_grad, w_in_grad, w_out_grad, kernel_grad)


def solution(mesh):
    return jax.shard_map(
        local,
        mesh=mesh,
        in_specs=(
            P("row", "dp", None, "col"),
            P("row", "dp", None, "col"),
            P(None, None, "col"),
            P("col", ("row", "dp")),
            P("row"),
            P("row"),
            P("row"),
            P(("row", "dp"), "col"),
        ),
        out_specs=(
            P("row", "dp", None, "col"),
            P("row", "dp", None, "col"),
            P("col", ("row", "dp")),
            P(("row", "dp"), "col"),
            P(None, None, "col"),
        ),
        check_vma=False,
    )
```

```python
import math

import jax
import jax.numpy as jnp
from jax import lax
from jax.experimental import pallas as pl
from jax.experimental.layout import Layout, with_layout_constraint
from jax.experimental.pallas import tpu as pltpu
from jax.sharding import PartitionSpec as P

epsilon = 1e-06
root_half = 0.7071067811865476
inv_root_tau = 0.3989422804014327
last_last = (((1,), (1,)), ((), ()))
f32 = jnp.float32
bf16 = jnp.bfloat16


def swap(block, axis, bits):
    count = lax.axis_size(axis)
    return lax.ppermute(block, axis, [(i, i ^ bits) for i in range(count)])


def pin(block):
    return with_layout_constraint(block, Layout(tuple(range(block.ndim))))


def after(blocks, *earlier):
    kept, _ = lax.optimization_barrier((blocks, earlier))
    return kept


def first_hops(block, every=False):
    count = lax.axis_size("col")
    bits = range(1, count) if every else [1 << i for i in range((count - 1).bit_length())]
    return {bit: pin(swap(block, "col", bit)) for bit in bits}


def gather_cols(block, hops):
    held = {0: pin(block)} | hops
    count = lax.axis_size("col")
    for m in sorted(range(1, count), key=lambda m: m.bit_count()):
        if m not in held:
            held[m] = pin(swap(held[m & (m - 1)], "col", m & -m))
    return [held[m] for m in range(count)]


def stack_cols(blocks):
    return [pin(jnp.stack([blocks[m] for m in side])) for side in col_order(len(blocks))]


def gather_rows(block, bits):
    held = {0: block}
    for bit in bits:
        held.update({q ^ bit: pin(swap(held[q], "row", bit)) for q in list(held)})
    return [held[q] for q in range(lax.axis_size("row"))]


def row_bits():
    return [1 << i for i in range((lax.axis_size("row") - 1).bit_length())]


def col_order(count):
    held, step = [0], count // 2
    while step > 1:
        held = held + [m ^ step for m in held]
        step //= 2
    return held, [m ^ 1 for m in held]


def halve_sum(near, far, axis, bits, earlier=()):
    for place, bit in enumerate(bits):
        got = swap(pin(far.astype(bf16)), axis, bit)
        if earlier:
            got = after(got, *earlier)
        total = near.astype(f32) + got.astype(f32)
        half = total.shape[0] // 2
        near, far = total[:half], total[half:]
    return total[0]


VMEM_BYTES = 44 * 2**20
in_vmem = pl.BlockSpec(memory_space=pltpu.VMEM)
in_smem = pl.BlockSpec(memory_space=pltpu.SMEM)


def call(body, outs, places, *operands):
    return pl.pallas_call(
        body,
        out_shape=outs,
        in_specs=[in_smem] + [in_vmem] * len(operands),
        out_specs=[in_vmem] * len(outs),
        compiler_params=pltpu.CompilerParams(vmem_limit_bytes=VMEM_BYTES),
        cost_estimate=pl.CostEstimate(flops=0, bytes_accessed=0, transcendentals=0),
    )(places, *operands)


def shape_of(dims, dtype):
    return jax.ShapeDtypeStruct(dims, dtype)


def piece_of(refs, places, rows, q, m):
    half = refs[-1].shape[-3] if len(refs) > 1 else refs[0].shape[1] // 2
    side, place = m // half, m % half
    if len(refs) == 1:
        return refs[0][places[0] ^ q, m]
    return refs[side * rows + q][place]


def cut_units(w, out, count):
    share = w.shape[1] // count
    for j in range(count):
        out[j] = w[:, j * share : (j + 1) * share]


def prepare(places, images, cotangent, w_in, reach):
    height, batch, width, chans = cotangent.shape
    count = lax.axis_size("col")
    span = height * width

    def body(places, images, cot, w_in, pieces, turned, low, high):
        cut_units(w_in, pieces, count)
        for b in range(batch):
            turned[:, b * span : (b + 1) * span] = cot[:, b].reshape(span, chans).T
        low[...] = images[height - reach :]
        high[...] = images[:reach]

    edge = shape_of((reach, batch, width, chans), bf16)
    outs = [
        shape_of((count, chans, w_in.shape[1] // count), bf16),
        shape_of((chans, batch * span), bf16),
        edge,
        edge,
    ]
    return call(body, outs, places, images, cotangent, w_in)


def prepare_out(places, w_out_turned):
    count = lax.axis_size("col")
    chans, units = w_out_turned.shape

    def body(places, w, pieces):
        cut_units(w, pieces, count)

    return call(body, [shape_of((count, chans, units // count), bf16)], places, w_out_turned)[0]


def join_weights(places, mine, other):
    count, chans, share = mine.shape
    units = 2 * share
    order = sum(col_order(count), [])

    def body(places, mine, other, out, turned):
        for place, m in enumerate(order):
            j = places[1] ^ m
            both = jnp.concatenate([mine[j], other[j]], axis=1)
            turned[place] = both
            out[place] = both.T

    outs = [shape_of((count, units, chans), bf16), shape_of((count, chans, units), bf16)]
    return call(body, outs, places, mine, other)


def image_sums(value, batch):
    span = value.shape[1] // batch
    return [jnp.sum(value[:, b * span : (b + 1) * span], axis=1, keepdims=True) for b in range(batch)]


def hidden_kernel(places, pieces, weights, bias, dims):
    rows, batch, pixels = dims
    count, units, chans = weights.shape

    def body(places, *refs):
        xs = refs[: len(pieces)]
        w, b, act, slope, square = refs[len(pieces) :]
        total = jnp.zeros((units, batch), f32)
        for q in range(rows):
            pre = b[...]
            for m in range(count):
                pre = pre + jnp.dot(w[m], piece_of(xs, places, rows, q, m), preferred_element_type=f32)
            cumul = 0.5 * (1.0 + lax.erf(pre * root_half))
            value = pre * cumul
            part = slice(q * pixels, (q + 1) * pixels)
            act[:, part] = value
            slope[:, part] = cumul + pre * jnp.exp(-0.5 * pre * pre) * inv_root_tau
            total = total + jnp.concatenate(image_sums(value * value, batch), axis=1)
        square[...] = total

    full = (units, rows * pixels)
    return call(
        body,
        [shape_of(full, f32), shape_of(full, f32), shape_of((units, batch), f32)],
        places,
        *pieces,
        weights,
        bias[:, None],
    )


def spread_images(vectors, units, span):
    count = vectors.shape[1]
    return jnp.concatenate(
        [jnp.broadcast_to(vectors[:, b : b + 1], (units, span)) for b in range(count)], axis=1
    )


def gated_kernel(places, act, gain, beta, dims):
    rows, batch, pixels = dims
    units = act.shape[0]

    def body(places, act, gain, beta, out):
        for q in range(rows):
            part = slice(q * pixels, (q + 1) * pixels)
            wide = spread_images(gain[...], units, pixels // batch)
            out[:, part] = (act[:, part] * wide + beta[...]).astype(bf16)

    return call(body, [shape_of(act.shape, bf16)], places, act, gain, beta)[0]


def back_kernel(places, pieces, weights, act, dims):
    rows, batch, pixels = dims
    count, units, chans = weights.shape

    def body(places, *refs):
        xs = refs[: len(pieces)]
        w, act, grad, pull = refs[len(pieces) :]
        total = jnp.zeros((units, batch), f32)
        for q in range(rows):
            value = jnp.zeros((units, pixels), f32)
            for m in range(count):
                value = value + jnp.dot(
                    w[m], piece_of(xs, places, rows, q, m), preferred_element_type=f32
                )
            part = slice(q * pixels, (q + 1) * pixels)
            grad[:, part] = value
            total = total + jnp.concatenate(image_sums(value * act[:, part], batch), axis=1)
        pull[...] = total

    return call(
        body,
        [shape_of(act.shape, f32), shape_of((units, batch), f32)],
        places,
        *pieces,
        weights,
        act,
    )


def project_kernel(places, made_of, operands, turned, dims, splits):
    rows, batch, pixels = dims
    count, chans, units = turned.shape
    half = count // 2

    def body(places, *refs):
        ins = refs[: len(operands)]
        w, kept = refs[len(operands) : len(operands) + 2]
        outs = refs[len(operands) + 2 :]

        def spread(vectors):
            return spread_images(vectors, units, pixels // batch)

        for q in range(rows):
            part = slice(q * pixels, (q + 1) * pixels)
            blocks = [r[:, part] if r.shape[1] == rows * pixels else r[...] for r in ins]
            made = made_of(blocks, spread).astype(bf16)
            kept[:, part] = made
            for m in range(count):
                value = jnp.dot(w[m], made, preferred_element_type=f32).astype(bf16)
                if not splits:
                    outs[0][places[0] ^ q, m] = value
                else:
                    side, place = m // half, m % half
                    bit = splits[side]
                    kind = 1 if q & bit else 0
                    outs[2 * side + kind][queue[side].index(q & ~bit), place] = value

    queue = [sorted({q & ~bit for q in range(rows)}) for bit in splits or []]
    if not splits:
        outs = [shape_of((rows, count, chans, pixels), bf16)]
    else:
        outs = [shape_of((rows // 2, half, chans, pixels), bf16)] * 4
    got = call(
        body, [shape_of((units, rows * pixels), bf16)] + outs, places, *operands, turned
    )
    return got[0], got[1:]


def grads_kernel(places, left, pieces, dims, count, chans):
    rows, batch, pixels = dims
    units = left.shape[0]
    share = units // 2
    order = sum(col_order(count), [])

    def body(places, left, *refs):
        xs = refs[: len(pieces)]
        mine, other = refs[len(pieces) :]
        for place, m in enumerate(order):
            x = jnp.concatenate([piece_of(xs, places, rows, q, place) for q in range(rows)], axis=1)
            value = lax.dot_general(x, left[...], last_last, preferred_element_type=f32).astype(bf16)
            mine[places[1] ^ m] = value[:, :share]
            other[places[1] ^ m] = value[:, share:]

    return call(body, [shape_of((count, chans, share), bf16)] * 2, places, left, *pieces)


def add_kernel(places, mine, got):
    def body(places, mine, got, out):
        for j in range(mine.shape[0]):
            out[j] = (mine[j].astype(f32) + got[j].astype(f32)).astype(bf16)

    return call(body, [shape_of(mine.shape, bf16)], places, mine, got)[0]


def finish_kernel(places, pieces, scale):
    count, chans, share = pieces.shape

    def body(places, pieces, out):
        wide = jnp.concatenate([pieces[j].astype(f32) for j in range(count)], axis=1)
        out[...] = wide * scale

    return call(body, [shape_of((chans, count * share), f32)], places, pieces)[0]


def own_units(vector):
    count = lax.axis_size("col")
    span = vector.shape[0] // 2
    share = span // count
    me = lax.axis_index("col")
    side = lax.axis_index("dp")
    mine = lax.dynamic_slice_in_dim(vector, side * span + me * share, share)
    other = lax.dynamic_slice_in_dim(vector, (1 - side) * span + me * share, share)
    return jnp.concatenate([mine, other])


def add_over(value, axis):
    n = lax.axis_size(axis)
    step = 1
    while step < n:
        value = value + swap(value, axis, step)
        step *= 2
    return value


def exchange_rows(low, high):
    count = lax.axis_size("row")
    forward = [(i, i + 1) for i in range(count - 1)]
    backward = [(i + 1, i) for i in range(count - 1)]
    return lax.ppermute(low, "row", forward), lax.ppermute(high, "row", backward)


EDGE = 8


def fill_padded(padded, low, mid, high):
    reach, height, width = low.shape[0], mid.shape[0], mid.shape[2]
    zeros = jnp.zeros(padded.shape[:2] + (EDGE, padded.shape[3]), f32)
    padded[:, :, :EDGE, :] = zeros
    padded[:, :, EDGE + width :, :] = zeros
    padded[:reach, :, EDGE : EDGE + width, :] = low[...].astype(f32)
    padded[reach : reach + height, :, EDGE : EDGE + width, :] = mid[...].astype(f32)
    padded[reach + height :, :, EDGE : EDGE + width, :] = high[...].astype(f32)


def lane_chunks(chans):
    return [slice(c, min(c + 128, chans)) for c in range(0, chans, 128)]


def depthwise(places, low, mid, high, kernel, extra, flip):
    height, batch, width, chans = mid.shape
    span = kernel.shape[0]
    reach = span // 2

    def body(places, low, mid, high, kern, *refs):
        out, padded = refs[-2:]
        fill_padded(padded, low, mid, high)

        @pl.loop(0, batch)
        def _(b):
            for lanes in lane_chunks(chans):
                sums = [None] * height
                for r in range(height + 2 * reach):
                    for j in range(span):
                        start = EDGE + j - reach
                        window = padded[r, b, start : start + width, lanes]
                        for h in range(max(0, r - span + 1), min(height, r + 1)):
                            i = r - h
                            tap = (span - 1 - i, span - 1 - j) if flip else (i, j)
                            term = kern[tap[0], tap[1] : tap[1] + 1, lanes] * window
                            sums[h] = term if sums[h] is None else sums[h] + term
                for h in range(height):
                    value = sums[h]
                    if extra is not None:
                        value = value + refs[0][h, b, :, lanes].astype(f32)
                    out[h, b, :, lanes] = value.astype(out.dtype)

    more = [] if extra is None else [extra]
    operands = [low, mid, high, kernel] + more
    return pl.pallas_call(
        body,
        out_shape=shape_of(mid.shape, f32 if extra is None else bf16),
        in_specs=[in_smem] + [in_vmem] * len(operands),
        out_specs=in_vmem,
        scratch_shapes=[pltpu.VMEM((height + 2 * reach, batch, width + 2 * EDGE, chans), f32)],
        compiler_params=pltpu.CompilerParams(vmem_limit_bytes=VMEM_BYTES),
        cost_estimate=pl.CostEstimate(flops=0, bytes_accessed=0, transcendentals=0),
    )(places, *operands)


def kernel_terms(places, low, mid, high, grad, span):
    height, batch, width, chans = mid.shape
    reach = span // 2

    def body(places, low, mid, high, grad, out, padded, sums):
        fill_padded(padded, low, mid, high)
        for lanes in lane_chunks(chans):
            for i in range(span):

                def step(b, total):
                    total = list(total)
                    for h in range(height):
                        piece = grad[h, b, :, lanes]
                        for j in range(span):
                            start = EDGE + j - reach
                            both = piece * padded[h + i, b, start : start + width, lanes]
                            total[j] = total[j] + jnp.sum(both.reshape(-1, 8, both.shape[1]), axis=0)
                    return tuple(total)

                zero = jnp.zeros((8, lanes.stop - lanes.start), f32)
                total = lax.fori_loop(0, batch, step, (zero,) * span)
                for j in range(span):
                    sums[i, j, :, lanes] = total[j]
        for i in range(span):
            out[i] = jnp.sum(sums[i], axis=1)

    operands = [low, mid, high, grad]
    return pl.pallas_call(
        body,
        out_shape=shape_of((span, span, chans), f32),
        in_specs=[in_smem] + [in_vmem] * len(operands),
        out_specs=in_vmem,
        scratch_shapes=[
            pltpu.VMEM((height + 2 * reach, batch, width + 2 * EDGE, chans), f32),
            pltpu.VMEM((span, span, 8, chans), f32),
        ],
        compiler_params=pltpu.CompilerParams(vmem_limit_bytes=VMEM_BYTES),
        cost_estimate=pl.CostEstimate(flops=0, bytes_accessed=0, transcendentals=0),
    )(places, *operands)


def local(images, cotangent, kernel, w_in, b_in, grn_gamma, grn_beta, w_out):
    height, batch, width, chans = images.shape
    span = kernel.shape[0]
    reach = span // 2
    col_count = lax.axis_size("col")
    row_count = lax.axis_size("row")
    all_chans = chans * col_count
    all_units = b_in.shape[0] * row_count
    pixels = height * batch * width
    group_pix = pixels * row_count
    scale_grad = 1.0 / math.sqrt(group_pix * lax.axis_size("dp"))

    places = jnp.stack([lax.axis_index("row"), lax.axis_index("col")]).astype(jnp.int32)
    dims = (row_count, batch, pixels)

    def turned(tile):
        return tile.transpose(3, 1, 0, 2).reshape(chans, pixels)

    def natural(block):
        return block.reshape(chans, batch, height, width).transpose(2, 1, 3, 0)


    pieces, cot_turned, low, high = prepare(places, images, cotangent, w_in, reach)
    cot_hops = first_hops(cot_turned, True)
    low, high = exchange_rows(low, high)
    bias, gamma, beta = own_units(b_in), own_units(grn_gamma), own_units(grn_beta)

    conv_out = depthwise(places, low, images, high, kernel, None, False)
    mean_own = jnp.mean(conv_out, axis=-1)
    dev_own = conv_out - mean_own[..., None]
    stats = jnp.stack([mean_own, jnp.sum(dev_own * dev_own, axis=-1)])
    cot_cols = after(gather_cols(cot_turned, cot_hops), stats)
    stats = [stats] + [swap(stats, "col", m) for m in range(1, col_count)]
    mean_pix = sum(s[0] for s in stats) / col_count
    var_pix = sum(s[1] + chans * (s[0] - mean_pix) ** 2 for s in stats) / all_chans
    inv_std = lax.rsqrt(var_pix + epsilon)[..., None]
    standard = (conv_out - mean_pix[..., None]) * inv_std
    bits = row_bits()
    normed = turned(standard.astype(bf16))
    normed_cols = gather_cols(normed, first_hops(normed))
    even, odd = stack_cols(normed_cols)
    normed_all = gather_rows(even, bits) + gather_rows(odd, bits[::-1])
    cot_all = [pin(lax.all_gather(pin(jnp.concatenate(stack_cols(cot_cols))), "row"))]
    w_in_there = lax.all_to_all(after(pieces, normed_cols), "col", 0, 0)
    near_rows = [normed_all[side + bit] for side in (0, row_count) for bit in bits]
    w_in_there = after(w_in_there, near_rows)
    w_in_all, w_in_turned = join_weights(places, w_in_there, swap(w_in_there, "dp", 1))
    pieces = after(prepare_out(places, w_out.T), w_in_there)
    w_out_there = lax.all_to_all(pieces, "col", 0, 0)
    act, slope, square = hidden_kernel(places, normed_all, w_in_all, bias, dims)
    norm_chan = jnp.sqrt(square + epsilon)
    norm_sum = add_over(add_over(jnp.sum(norm_chan, axis=0), "row"), "col")
    denom = norm_sum / all_units + epsilon
    gamma, beta = gamma[:, None], beta[:, None]
    gain = gamma * (norm_chan / denom) + 1.0
    gated = gated_kernel(places, act, gain, beta, dims)
    w_out_mine, w_out_other = grads_kernel(places, gated, cot_all, dims, col_count, chans)
    w_out_sums = add_kernel(places, w_out_mine, swap(w_out_other, "dp", 1))
    w_out_there = after(w_out_there, w_out_sums)
    w_out_all, w_out_turned = join_weights(places, w_out_there, swap(w_out_there, "dp", 1))
    w_out_back = lax.all_to_all(after(w_out_sums, w_out_there), "col", 0, 0)
    w_out_grad = finish_kernel(places, w_out_back, scale_grad).T
    grad_gated, pull = back_kernel(places, cot_all, w_out_all, act, dims)
    share_back = gamma * pull / denom / norm_chan

    grad_pre, grad_parts = project_kernel(
        places,
        lambda b, spread: (b[0] * spread(b[3]) + b[1] * spread(b[4])) * b[2],
        [grad_gated, act, slope, gain, share_back],
        w_in_turned,
        dims,
        (bits[0], bits[-1]),
    )
    _, out_parts = project_kernel(
        places, lambda b, spread: b[0], [gated], w_out_turned, dims, (bits[0], bits[-1])
    )
    w_in_mine, w_in_other = grads_kernel(places, grad_pre, normed_all, dims, col_count, chans)
    w_in_sums = add_kernel(places, w_in_mine, swap(w_in_other, "dp", 1))

    near_a, far_a, near_b, far_b = grad_parts
    even = halve_sum(near_a, far_a, "row", bits, (w_in_other, out_parts[0]))
    odd = halve_sum(near_b, far_b, "row", bits[::-1], (w_in_other, out_parts[0]))
    down = [1 << i for i in range((col_count - 1).bit_length())]
    near_a, far_a, near_b, far_b = out_parts
    far_a, far_b = after((far_a, far_b), even, odd)
    out_even = halve_sum(near_a, far_a, "row", bits)
    out_odd = halve_sum(near_b, far_b, "row", bits[::-1])
    odd = after(odd, w_out_back)
    grad_normed = natural(pin(halve_sum(even, odd, "col", down)))

    sums = jnp.stack([jnp.sum(grad_normed, axis=-1), jnp.sum(grad_normed * standard, axis=-1)])
    sums = sum([swap(sums, "col", m) for m in range(1, col_count)], sums) / all_chans
    out_odd = after(out_odd, sums)
    w_in_back = lax.all_to_all(after(w_in_sums, sums), "col", 0, 0)
    w_in_grad = finish_kernel(places, w_in_back, scale_grad)
    grad_conv = inv_std * (grad_normed - sums[0][..., None] - standard * sums[1][..., None])
    edge = grad_conv.astype(bf16)
    low_grad, high_grad = exchange_rows(edge[height - reach :], edge[:reach])
    x_grad = depthwise(places, low_grad, grad_conv, high_grad, kernel, cotangent, True)
    kern = kernel_terms(places, low, images, high, after(grad_conv, low_grad, high_grad), span)
    steps = [("dp", 1)] + [("row", 1 << i) for i in range((row_count - 1).bit_length())]
    for axis, step in steps:
        kern = kern.astype(bf16)
        kern = kern.astype(f32) + swap(kern, axis, step).astype(f32)
    kernel_grad = kern * scale_grad
    branch = halve_sum(out_even, out_odd, "col", down, (x_grad,))
    branch = natural(pin(branch))
    result = (images.astype(f32) + branch.astype(f32)).astype(bf16)
    return (result, x_grad, w_in_grad, w_out_grad, kernel_grad)


def solution(mesh):
    return jax.shard_map(
        local,
        mesh=mesh,
        in_specs=(
            P("row", "dp", None, "col"),
            P("row", "dp", None, "col"),
            P(None, None, "col"),
            P("col", ("row", "dp")),
            P("row"),
            P("row"),
            P("row"),
            P(("row", "dp"), "col"),
        ),
        out_specs=(
            P("row", "dp", None, "col"),
            P("row", "dp", None, "col"),
            P("col", ("row", "dp")),
            P(("row", "dp"), "col"),
            P(None, None, "col"),
        ),
        check_vma=False,
    )
```

```python
import math

import jax
import jax.numpy as jnp
from jax import lax
from jax.experimental import pallas as pl
from jax.experimental.layout import Layout, with_layout_constraint
from jax.experimental.pallas import tpu as pltpu
from jax.sharding import PartitionSpec as P

epsilon = 1e-06
root_half = 0.7071067811865476
inv_root_tau = 0.3989422804014327
last_last = (((1,), (1,)), ((), ()))
f32 = jnp.float32
bf16 = jnp.bfloat16


def swap(block, axis, bits):
    count = lax.axis_size(axis)
    return lax.ppermute(block, axis, [(i, i ^ bits) for i in range(count)])


def pin(block):
    return with_layout_constraint(block, Layout(tuple(range(block.ndim))))


def after(blocks, *earlier):
    kept, _ = lax.optimization_barrier((blocks, earlier))
    return kept


def first_hops(block, every=False):
    count = lax.axis_size("col")
    bits = range(1, count) if every else [1 << i for i in range((count - 1).bit_length())]
    return {bit: pin(swap(block, "col", bit)) for bit in bits}


def gather_cols(block, hops):
    held = {0: pin(block)} | hops
    count = lax.axis_size("col")
    for m in sorted(range(1, count), key=lambda m: m.bit_count()):
        if m not in held:
            held[m] = pin(swap(held[m & (m - 1)], "col", m & -m))
    return [held[m] for m in range(count)]


def stack_cols(blocks):
    return pin(jnp.stack([blocks[m] for side in col_order(len(blocks)) for m in side]))


def gather_rows(stacked):
    half = stacked.shape[0] // 2
    one = pin(swap(stacked, "row", 1))
    two = pin(swap(stacked, "row", 2))
    return [
        stacked,
        one,
        two,
        pin(swap(pin(one[:half]), "row", 2)),
        pin(swap(pin(two[half:]), "row", 1)),
    ]


def row_bits():
    return [1 << i for i in range((lax.axis_size("row") - 1).bit_length())]


def col_order(count):
    held, step = [0], count // 2
    while step > 1:
        held = held + [m ^ step for m in held]
        step //= 2
    return held, [m ^ 1 for m in held]


def halve_sum(near, far, axis, bits, earlier=()):
    for bit in bits:
        got = swap(pin(far.astype(bf16)), axis, bit)
        if earlier:
            got = after(got, *earlier)
        total = near.astype(f32) + got.astype(f32)
        half = total.shape[0] // 2
        near, far = total[:half], total[half:]
    return total[0]


VMEM_BYTES = 44 * 2**20
in_vmem = pl.BlockSpec(memory_space=pltpu.VMEM)
in_smem = pl.BlockSpec(memory_space=pltpu.SMEM)


def call(body, outs, places, *operands):
    return pl.pallas_call(
        body,
        out_shape=outs,
        in_specs=[in_smem] + [in_vmem] * len(operands),
        out_specs=[in_vmem] * len(outs),
        compiler_params=pltpu.CompilerParams(vmem_limit_bytes=VMEM_BYTES),
        cost_estimate=pl.CostEstimate(flops=0, bytes_accessed=0, transcendentals=0),
    )(places, *operands)


def shape_of(dims, dtype):
    return jax.ShapeDtypeStruct(dims, dtype)


def piece_of(refs, places, rows, q, m):
    if q < rows - 1:
        return refs[q][m]
    half = refs[-1].shape[0]
    return refs[rows - 1 + m // half][m % half]


def cut_units(w, out, count):
    share = w.shape[1] // count
    for j in range(count):
        out[j] = w[:, j * share : (j + 1) * share]


def prepare(places, images, cotangent, w_in, reach):
    height, batch, width, chans = cotangent.shape
    count = lax.axis_size("col")
    span = height * width

    def body(places, images, cot, w_in, pieces, turned, low, high):
        cut_units(w_in, pieces, count)
        for b in range(batch):
            turned[:, b * span : (b + 1) * span] = cot[:, b].reshape(span, chans).T
        low[...] = images[height - reach :]
        high[...] = images[:reach]

    edge = shape_of((reach, batch, width, chans), bf16)
    outs = [
        shape_of((count, chans, w_in.shape[1] // count), bf16),
        shape_of((chans, batch * span), bf16),
        edge,
        edge,
    ]
    return call(body, outs, places, images, cotangent, w_in)


def prepare_out(places, w_out_turned):
    count = lax.axis_size("col")
    chans, units = w_out_turned.shape

    def body(places, w, pieces):
        cut_units(w, pieces, count)

    return call(body, [shape_of((count, chans, units // count), bf16)], places, w_out_turned)[0]


def join_weights(places, mine, other):
    count, chans, share = mine.shape
    units = 2 * share
    order = sum(col_order(count), [])

    def body(places, mine, other, out, turned):
        for place, m in enumerate(order):
            j = places[1] ^ m
            both = jnp.concatenate([mine[j], other[j]], axis=1)
            turned[place] = both
            out[place] = both.T

    outs = [shape_of((count, units, chans), bf16), shape_of((count, chans, units), bf16)]
    return call(body, outs, places, mine, other)


def image_sums(value, batch):
    span = value.shape[1] // batch
    return [jnp.sum(value[:, b * span : (b + 1) * span], axis=1, keepdims=True) for b in range(batch)]


def hidden_kernel(places, pieces, weights, bias, dims):
    rows, batch, pixels = dims
    count, units, chans = weights.shape

    def body(places, *refs):
        xs = refs[: len(pieces)]
        w, b, act, slope, square = refs[len(pieces) :]
        total = jnp.zeros((units, batch), f32)
        for q in range(rows):
            pre = b[...]
            for m in range(count):
                pre = pre + jnp.dot(w[m], piece_of(xs, places, rows, q, m), preferred_element_type=f32)
            cumul = 0.5 * (1.0 + lax.erf(pre * root_half))
            value = pre * cumul
            part = slice(q * pixels, (q + 1) * pixels)
            act[:, part] = value
            slope[:, part] = cumul + pre * jnp.exp(-0.5 * pre * pre) * inv_root_tau
            total = total + jnp.concatenate(image_sums(value * value, batch), axis=1)
        square[...] = total

    full = (units, rows * pixels)
    return call(
        body,
        [shape_of(full, f32), shape_of(full, f32), shape_of((units, batch), f32)],
        places,
        *pieces,
        weights,
        bias[:, None],
    )


def spread_images(vectors, units, span):
    count = vectors.shape[1]
    return jnp.concatenate(
        [jnp.broadcast_to(vectors[:, b : b + 1], (units, span)) for b in range(count)], axis=1
    )


def gated_kernel(places, act, gain, beta, dims):
    rows, batch, pixels = dims
    units = act.shape[0]

    def body(places, act, gain, beta, out):
        for q in range(rows):
            part = slice(q * pixels, (q + 1) * pixels)
            wide = spread_images(gain[...], units, pixels // batch)
            out[:, part] = (act[:, part] * wide + beta[...]).astype(bf16)

    return call(body, [shape_of(act.shape, bf16)], places, act, gain, beta)[0]


def back_kernel(places, pieces, weights, act, dims):
    rows, batch, pixels = dims
    count, units, chans = weights.shape

    def body(places, *refs):
        xs = refs[: len(pieces)]
        w, act, grad, pull = refs[len(pieces) :]
        total = jnp.zeros((units, batch), f32)
        for q in range(rows):
            value = jnp.zeros((units, pixels), f32)
            for m in range(count):
                value = value + jnp.dot(
                    w[m], piece_of(xs, places, rows, q, m), preferred_element_type=f32
                )
            part = slice(q * pixels, (q + 1) * pixels)
            grad[:, part] = value
            total = total + jnp.concatenate(image_sums(value * act[:, part], batch), axis=1)
        pull[...] = total

    return call(
        body,
        [shape_of(act.shape, f32), shape_of((units, batch), f32)],
        places,
        *pieces,
        weights,
        act,
    )


def project_kernel(places, made_of, operands, turned, dims, splits):
    rows, batch, pixels = dims
    count, chans, units = turned.shape
    half = count // 2

    def body(places, *refs):
        ins = refs[: len(operands)]
        w, kept = refs[len(operands) : len(operands) + 2]
        outs = refs[len(operands) + 2 :]

        def spread(vectors):
            return spread_images(vectors, units, pixels // batch)

        for q in range(rows):
            part = slice(q * pixels, (q + 1) * pixels)
            blocks = [r[:, part] if r.shape[1] == rows * pixels else r[...] for r in ins]
            made = made_of(blocks, spread).astype(bf16)
            kept[:, part] = made
            for m in range(count):
                value = jnp.dot(w[m], made, preferred_element_type=f32).astype(bf16)
                if not splits:
                    outs[0][places[0] ^ q, m] = value
                else:
                    side, place = m // half, m % half
                    bit = splits[side]
                    kind = 1 if q & bit else 0
                    outs[2 * side + kind][queue[side].index(q & ~bit), place] = value

    queue = [sorted({q & ~bit for q in range(rows)}) for bit in splits or []]
    if not splits:
        outs = [shape_of((rows, count, chans, pixels), bf16)]
    else:
        outs = [shape_of((rows // 2, half, chans, pixels), bf16)] * 4
    got = call(
        body, [shape_of((units, rows * pixels), bf16)] + outs, places, *operands, turned
    )
    return got[0], got[1:]


def grads_kernel(places, left, pieces, dims, count, chans):
    rows, batch, pixels = dims
    units = left.shape[0]
    share = units // 2
    order = sum(col_order(count), [])

    def body(places, left, *refs):
        xs = refs[: len(pieces)]
        mine, other = refs[len(pieces) :]
        for place, m in enumerate(order):
            x = jnp.concatenate([piece_of(xs, places, rows, q, place) for q in range(rows)], axis=1)
            value = lax.dot_general(x, left[...], last_last, preferred_element_type=f32).astype(bf16)
            mine[places[1] ^ m] = value[:, :share]
            other[places[1] ^ m] = value[:, share:]

    return call(body, [shape_of((count, chans, share), bf16)] * 2, places, left, *pieces)


def add_kernel(places, mine, got):
    def body(places, mine, got, out):
        for j in range(mine.shape[0]):
            out[j] = (mine[j].astype(f32) + got[j].astype(f32)).astype(bf16)

    return call(body, [shape_of(mine.shape, bf16)], places, mine, got)[0]


def finish_kernel(places, pieces, scale):
    count, chans, share = pieces.shape

    def body(places, pieces, out):
        wide = jnp.concatenate([pieces[j].astype(f32) for j in range(count)], axis=1)
        out[...] = wide * scale

    return call(body, [shape_of((chans, count * share), f32)], places, pieces)[0]


def own_units(vector):
    count = lax.axis_size("col")
    span = vector.shape[0] // 2
    share = span // count
    me = lax.axis_index("col")
    side = lax.axis_index("dp")
    mine = lax.dynamic_slice_in_dim(vector, side * span + me * share, share)
    other = lax.dynamic_slice_in_dim(vector, (1 - side) * span + me * share, share)
    return jnp.concatenate([mine, other])


def add_over(value, axis):
    n = lax.axis_size(axis)
    step = 1
    while step < n:
        value = value + swap(value, axis, step)
        step *= 2
    return value


def exchange_rows(low, high):
    count = lax.axis_size("row")
    forward = [(i, i + 1) for i in range(count - 1)]
    backward = [(i + 1, i) for i in range(count - 1)]
    return lax.ppermute(low, "row", forward), lax.ppermute(high, "row", backward)


EDGE = 8


def fill_padded(padded, low, mid, high):
    reach, height, width = low.shape[0], mid.shape[0], mid.shape[2]
    zeros = jnp.zeros(padded.shape[:2] + (EDGE, padded.shape[3]), f32)
    padded[:, :, :EDGE, :] = zeros
    padded[:, :, EDGE + width :, :] = zeros
    padded[:reach, :, EDGE : EDGE + width, :] = low[...].astype(f32)
    padded[reach : reach + height, :, EDGE : EDGE + width, :] = mid[...].astype(f32)
    padded[reach + height :, :, EDGE : EDGE + width, :] = high[...].astype(f32)


def lane_chunks(chans):
    return [slice(c, min(c + 128, chans)) for c in range(0, chans, 128)]


def depthwise(places, low, mid, high, kernel, extra, flip):
    height, batch, width, chans = mid.shape
    span = kernel.shape[0]
    reach = span // 2

    def body(places, low, mid, high, kern, *refs):
        out, padded = refs[-2:]
        fill_padded(padded, low, mid, high)

        @pl.loop(0, batch)
        def _(b):
            for lanes in lane_chunks(chans):
                sums = [None] * height
                for r in range(height + 2 * reach):
                    for j in range(span):
                        start = EDGE + j - reach
                        window = padded[r, b, start : start + width, lanes]
                        for h in range(max(0, r - span + 1), min(height, r + 1)):
                            i = r - h
                            tap = (span - 1 - i, span - 1 - j) if flip else (i, j)
                            term = kern[tap[0], tap[1] : tap[1] + 1, lanes] * window
                            sums[h] = term if sums[h] is None else sums[h] + term
                for h in range(height):
                    value = sums[h]
                    if extra is not None:
                        value = value + refs[0][h, b, :, lanes].astype(f32)
                    out[h, b, :, lanes] = value.astype(out.dtype)

    more = [] if extra is None else [extra]
    operands = [low, mid, high, kernel] + more
    return pl.pallas_call(
        body,
        out_shape=shape_of(mid.shape, f32 if extra is None else bf16),
        in_specs=[in_smem] + [in_vmem] * len(operands),
        out_specs=in_vmem,
        scratch_shapes=[pltpu.VMEM((height + 2 * reach, batch, width + 2 * EDGE, chans), f32)],
        compiler_params=pltpu.CompilerParams(vmem_limit_bytes=VMEM_BYTES),
        cost_estimate=pl.CostEstimate(flops=0, bytes_accessed=0, transcendentals=0),
    )(places, *operands)


def kernel_terms(places, low, mid, high, grad, span):
    height, batch, width, chans = mid.shape
    reach = span // 2

    def body(places, low, mid, high, grad, out, padded, sums):
        fill_padded(padded, low, mid, high)
        for lanes in lane_chunks(chans):
            for i in range(span):

                def step(b, total):
                    total = list(total)
                    for h in range(height):
                        piece = grad[h, b, :, lanes]
                        for j in range(span):
                            start = EDGE + j - reach
                            both = piece * padded[h + i, b, start : start + width, lanes]
                            total[j] = total[j] + jnp.sum(both.reshape(-1, 8, both.shape[1]), axis=0)
                    return tuple(total)

                zero = jnp.zeros((8, lanes.stop - lanes.start), f32)
                total = lax.fori_loop(0, batch, step, (zero,) * span)
                for j in range(span):
                    sums[i, j, :, lanes] = total[j]
        for i in range(span):
            out[i] = jnp.sum(sums[i], axis=1)

    operands = [low, mid, high, grad]
    return pl.pallas_call(
        body,
        out_shape=shape_of((span, span, chans), f32),
        in_specs=[in_smem] + [in_vmem] * len(operands),
        out_specs=in_vmem,
        scratch_shapes=[
            pltpu.VMEM((height + 2 * reach, batch, width + 2 * EDGE, chans), f32),
            pltpu.VMEM((span, span, 8, chans), f32),
        ],
        compiler_params=pltpu.CompilerParams(vmem_limit_bytes=VMEM_BYTES),
        cost_estimate=pl.CostEstimate(flops=0, bytes_accessed=0, transcendentals=0),
    )(places, *operands)


def local(images, cotangent, kernel, w_in, b_in, grn_gamma, grn_beta, w_out):
    height, batch, width, chans = images.shape
    span = kernel.shape[0]
    reach = span // 2
    col_count = lax.axis_size("col")
    row_count = lax.axis_size("row")
    all_chans = chans * col_count
    all_units = b_in.shape[0] * row_count
    pixels = height * batch * width
    group_pix = pixels * row_count
    scale_grad = 1.0 / math.sqrt(group_pix * lax.axis_size("dp"))

    places = jnp.stack([lax.axis_index("row"), lax.axis_index("col")]).astype(jnp.int32)
    dims = (row_count, batch, pixels)

    def turned(tile):
        return tile.transpose(3, 1, 0, 2).reshape(chans, pixels)

    def natural(block):
        return block.reshape(chans, batch, height, width).transpose(2, 1, 3, 0)


    pieces, cot_turned, low, high = prepare(places, images, cotangent, w_in, reach)
    cot_hops = first_hops(cot_turned, True)
    low, high = exchange_rows(low, high)
    bias, gamma, beta = own_units(b_in), own_units(grn_gamma), own_units(grn_beta)

    conv_out = depthwise(places, low, images, high, kernel, None, False)
    mean_own = jnp.mean(conv_out, axis=-1)
    dev_own = conv_out - mean_own[..., None]
    stats = jnp.stack([mean_own, jnp.sum(dev_own * dev_own, axis=-1)])
    stats = after(stats, cot_hops)
    cot_all = gather_rows(stack_cols(gather_cols(cot_turned, cot_hops)))
    stats = [stats] + [swap(stats, "col", m) for m in range(1, col_count)]
    mean_pix = sum(s[0] for s in stats) / col_count
    var_pix = sum(s[1] + chans * (s[0] - mean_pix) ** 2 for s in stats) / all_chans
    inv_std = lax.rsqrt(var_pix + epsilon)[..., None]
    standard = (conv_out - mean_pix[..., None]) * inv_std
    bits = row_bits()
    normed = turned(standard.astype(bf16))
    normed_cols = gather_cols(normed, first_hops(normed))
    normed_stack = after(stack_cols(normed_cols), cot_all[1], cot_all[2])
    normed_all = gather_rows(normed_stack)
    w_in_there = lax.all_to_all(after(pieces, normed_stack), "col", 0, 0)
    w_in_there = after(w_in_there, normed_all[1], normed_all[2], cot_all[3], cot_all[4])
    w_in_all, w_in_turned = join_weights(places, w_in_there, swap(w_in_there, "dp", 1))
    pieces = after(prepare_out(places, w_out.T), w_in_there)
    w_out_there = lax.all_to_all(pieces, "col", 0, 0)
    act, slope, square = hidden_kernel(places, normed_all, w_in_all, bias, dims)
    norm_chan = jnp.sqrt(square + epsilon)
    norm_sum = add_over(add_over(jnp.sum(norm_chan, axis=0), "row"), "col")
    denom = norm_sum / all_units + epsilon
    gamma, beta = gamma[:, None], beta[:, None]
    gain = gamma * (norm_chan / denom) + 1.0
    gated = gated_kernel(places, act, gain, beta, dims)
    w_out_mine, w_out_other = grads_kernel(places, gated, cot_all, dims, col_count, chans)
    w_out_sums = add_kernel(places, w_out_mine, swap(w_out_other, "dp", 1))
    w_out_there = after(w_out_there, w_out_sums)
    w_out_back = lax.all_to_all(after(w_out_sums, w_out_there), "col", 0, 0)
    w_out_grad = finish_kernel(places, w_out_back, scale_grad).T
    w_out_all, w_out_turned = join_weights(places, w_out_there, swap(w_out_there, "dp", 1))
    grad_gated, pull = back_kernel(places, cot_all, w_out_all, act, dims)
    share_back = gamma * pull / denom / norm_chan

    grad_pre, grad_parts = project_kernel(
        places,
        lambda b, spread: (b[0] * spread(b[3]) + b[1] * spread(b[4])) * b[2],
        [grad_gated, act, slope, gain, share_back],
        w_in_turned,
        dims,
        (bits[0], bits[-1]),
    )
    _, out_parts = project_kernel(
        places, lambda b, spread: b[0], [gated], w_out_turned, dims, (bits[0], bits[-1])
    )
    w_in_mine, w_in_other = grads_kernel(
        places, grad_pre, normed_all, dims, col_count, chans
    )
    w_in_sums = add_kernel(places, w_in_mine, swap(w_in_other, "dp", 1))

    near_a, far_a, near_b, far_b = grad_parts
    shade = (w_in_other, out_parts[0])
    even = halve_sum(near_a, far_a, "row", bits, shade)
    odd = halve_sum(near_b, far_b, "row", bits[::-1], shade)
    down = [1 << i for i in range((col_count - 1).bit_length())]
    near_a, far_a, near_b, far_b = out_parts
    far_a, far_b = after((far_a, far_b), even, odd)
    out_even = halve_sum(near_a, far_a, "row", bits)
    out_odd = halve_sum(near_b, far_b, "row", bits[::-1])
    odd = after(odd, w_out_back)
    grad_normed = natural(pin(halve_sum(even, odd, "col", down)))

    sums = jnp.stack([jnp.sum(grad_normed, axis=-1), jnp.sum(grad_normed * standard, axis=-1)])
    sums = sum([swap(sums, "col", m) for m in range(1, col_count)], sums) / all_chans
    out_odd = after(out_odd, sums)
    w_in_back = lax.all_to_all(after(w_in_sums, sums), "col", 0, 0)
    w_in_grad = finish_kernel(places, w_in_back, scale_grad)
    grad_conv = inv_std * (grad_normed - sums[0][..., None] - standard * sums[1][..., None])
    edge = grad_conv.astype(bf16)
    low_grad, high_grad = exchange_rows(edge[height - reach :], edge[:reach])
    x_grad = depthwise(places, low_grad, grad_conv, high_grad, kernel, cotangent, True)
    kern = kernel_terms(places, low, images, high, after(grad_conv, low_grad, high_grad), span)
    steps = [("dp", 1)] + [("row", 1 << i) for i in range((row_count - 1).bit_length())]
    for axis, step in steps:
        kern = kern.astype(bf16)
        kern = kern.astype(f32) + swap(kern, axis, step).astype(f32)
    kernel_grad = kern * scale_grad
    branch = halve_sum(out_even, out_odd, "col", down, (x_grad,))
    branch = natural(pin(branch))
    result = (images.astype(f32) + branch.astype(f32)).astype(bf16)
    return (result, x_grad, w_in_grad, w_out_grad, kernel_grad)


def solution(mesh):
    return jax.shard_map(
        local,
        mesh=mesh,
        in_specs=(
            P("row", "dp", None, "col"),
            P("row", "dp", None, "col"),
            P(None, None, "col"),
            P("col", ("row", "dp")),
            P("row"),
            P("row"),
            P("row"),
            P(("row", "dp"), "col"),
        ),
        out_specs=(
            P("row", "dp", None, "col"),
            P("row", "dp", None, "col"),
            P("col", ("row", "dp")),
            P(("row", "dp"), "col"),
            P(None, None, "col"),
        ),
        check_vma=False,
    )
```

```python
import math

import jax
import jax.numpy as jnp
from jax import lax
from jax.experimental import pallas as pl
from jax.experimental.layout import Layout, with_layout_constraint
from jax.experimental.pallas import tpu as pltpu
from jax.sharding import PartitionSpec as P

epsilon = 1e-06
root_half = 0.7071067811865476
inv_root_tau = 0.3989422804014327
last_last = (((1,), (1,)), ((), ()))
f32 = jnp.float32
bf16 = jnp.bfloat16


def swap(block, axis, bits):
    count = lax.axis_size(axis)
    return lax.ppermute(block, axis, [(i, i ^ bits) for i in range(count)])


def pin(block):
    return with_layout_constraint(block, Layout(tuple(range(block.ndim))))


def after(blocks, *earlier):
    kept, _ = lax.optimization_barrier((blocks, earlier))
    return kept


def first_hops(block, every=False):
    count = lax.axis_size("col")
    bits = range(1, count) if every else [1 << i for i in range((count - 1).bit_length())]
    return {bit: pin(swap(block, "col", bit)) for bit in bits}


def gather_cols(block, hops):
    held = {0: pin(block)} | hops
    count = lax.axis_size("col")
    for m in sorted(range(1, count), key=lambda m: m.bit_count()):
        if m not in held:
            held[m] = pin(swap(held[m & (m - 1)], "col", m & -m))
    return [held[m] for m in range(count)]


def stack_cols(blocks):
    return pin(jnp.stack([blocks[m] for side in col_order(len(blocks)) for m in side]))


def gather_rows(stacked):
    half = stacked.shape[0] // 2
    one = pin(swap(stacked, "row", 1))
    two = pin(swap(stacked, "row", 2))
    return [
        stacked,
        one,
        two,
        pin(swap(pin(one[:half]), "row", 2)),
        pin(swap(pin(two[half:]), "row", 1)),
    ]


def row_bits():
    return [1 << i for i in range((lax.axis_size("row") - 1).bit_length())]


def col_order(count):
    held, step = [0], count // 2
    while step > 1:
        held = held + [m ^ step for m in held]
        step //= 2
    return held, [m ^ 1 for m in held]


def halve_sum(near, far, axis, bits, earlier=()):
    for bit in bits:
        got = swap(pin(far.astype(bf16)), axis, bit)
        if earlier:
            got = after(got, *earlier)
        total = near.astype(f32) + got.astype(f32)
        half = total.shape[0] // 2
        near, far = total[:half], total[half:]
    return total[0]


VMEM_BYTES = 44 * 2**20
in_vmem = pl.BlockSpec(memory_space=pltpu.VMEM)
in_smem = pl.BlockSpec(memory_space=pltpu.SMEM)


def call(body, outs, places, *operands):
    return pl.pallas_call(
        body,
        out_shape=outs,
        in_specs=[in_smem] + [in_vmem] * len(operands),
        out_specs=[in_vmem] * len(outs),
        compiler_params=pltpu.CompilerParams(vmem_limit_bytes=VMEM_BYTES),
        cost_estimate=pl.CostEstimate(flops=0, bytes_accessed=0, transcendentals=0),
    )(places, *operands)


def shape_of(dims, dtype):
    return jax.ShapeDtypeStruct(dims, dtype)


def piece_of(refs, places, rows, q, m):
    if q < rows - 1:
        return refs[q][m]
    half = refs[-1].shape[0]
    return refs[rows - 1 + m // half][m % half]


def cut_units(w, out, count):
    share = w.shape[1] // count
    for j in range(count):
        out[j] = w[:, j * share : (j + 1) * share]


def prepare(places, images, cotangent, w_in, reach):
    height, batch, width, chans = cotangent.shape
    count = lax.axis_size("col")
    span = height * width

    def body(places, images, cot, w_in, pieces, turned, low, high):
        cut_units(w_in, pieces, count)
        for b in range(batch):
            turned[:, b * span : (b + 1) * span] = cot[:, b].reshape(span, chans).T
        low[...] = images[height - reach :]
        high[...] = images[:reach]

    edge = shape_of((reach, batch, width, chans), bf16)
    outs = [
        shape_of((count, chans, w_in.shape[1] // count), bf16),
        shape_of((chans, batch * span), bf16),
        edge,
        edge,
    ]
    return call(body, outs, places, images, cotangent, w_in)


def prepare_out(places, w_out_turned):
    count = lax.axis_size("col")
    chans, units = w_out_turned.shape

    def body(places, w, pieces):
        cut_units(w, pieces, count)

    return call(body, [shape_of((count, chans, units // count), bf16)], places, w_out_turned)[0]


def join_weights(places, mine, other):
    count, chans, share = mine.shape
    units = 2 * share
    order = sum(col_order(count), [])

    def body(places, mine, other, out, turned):
        for place, m in enumerate(order):
            j = places[1] ^ m
            both = jnp.concatenate([mine[j], other[j]], axis=1)
            turned[place] = both
            out[place] = both.T

    outs = [shape_of((count, units, chans), bf16), shape_of((count, chans, units), bf16)]
    return call(body, outs, places, mine, other)


def image_sums(value, batch):
    span = value.shape[1] // batch
    return [jnp.sum(value[:, b * span : (b + 1) * span], axis=1, keepdims=True) for b in range(batch)]


def hidden_kernel(places, pieces, weights, bias, dims):
    rows, batch, pixels = dims
    count, units, chans = weights.shape

    def body(places, *refs):
        xs = refs[: len(pieces)]
        w, b, act, slope, square = refs[len(pieces) :]
        total = jnp.zeros((units, batch), f32)
        for q in range(rows):
            pre = b[...]
            for m in range(count):
                pre = pre + jnp.dot(w[m], piece_of(xs, places, rows, q, m), preferred_element_type=f32)
            cumul = 0.5 * (1.0 + lax.erf(pre * root_half))
            value = pre * cumul
            part = slice(q * pixels, (q + 1) * pixels)
            act[:, part] = value
            slope[:, part] = cumul + pre * jnp.exp(-0.5 * pre * pre) * inv_root_tau
            total = total + jnp.concatenate(image_sums(value * value, batch), axis=1)
        square[...] = total

    full = (units, rows * pixels)
    return call(
        body,
        [shape_of(full, f32), shape_of(full, f32), shape_of((units, batch), f32)],
        places,
        *pieces,
        weights,
        bias[:, None],
    )


def spread_images(vectors, units, span):
    count = vectors.shape[1]
    return jnp.concatenate(
        [jnp.broadcast_to(vectors[:, b : b + 1], (units, span)) for b in range(count)], axis=1
    )


def gated_kernel(places, act, gain, beta, dims):
    rows, batch, pixels = dims
    units = act.shape[0]

    def body(places, act, gain, beta, out):
        for q in range(rows):
            part = slice(q * pixels, (q + 1) * pixels)
            wide = spread_images(gain[...], units, pixels // batch)
            out[:, part] = (act[:, part] * wide + beta[...]).astype(bf16)

    return call(body, [shape_of(act.shape, bf16)], places, act, gain, beta)[0]


def back_kernel(places, pieces, weights, act, dims):
    rows, batch, pixels = dims
    count, units, chans = weights.shape

    def body(places, *refs):
        xs = refs[: len(pieces)]
        w, act, grad, pull = refs[len(pieces) :]
        total = jnp.zeros((units, batch), f32)
        for q in range(rows):
            value = jnp.zeros((units, pixels), f32)
            for m in range(count):
                value = value + jnp.dot(
                    w[m], piece_of(xs, places, rows, q, m), preferred_element_type=f32
                )
            part = slice(q * pixels, (q + 1) * pixels)
            grad[:, part] = value
            total = total + jnp.concatenate(image_sums(value * act[:, part], batch), axis=1)
        pull[...] = total

    return call(
        body,
        [shape_of(act.shape, f32), shape_of((units, batch), f32)],
        places,
        *pieces,
        weights,
        act,
    )


def project_kernel(places, made_of, operands, turned, dims, splits):
    rows, batch, pixels = dims
    count, chans, units = turned.shape
    half = count // 2

    def body(places, *refs):
        ins = refs[: len(operands)]
        w, kept = refs[len(operands) : len(operands) + 2]
        outs = refs[len(operands) + 2 :]

        def spread(vectors):
            return spread_images(vectors, units, pixels // batch)

        for q in range(rows):
            part = slice(q * pixels, (q + 1) * pixels)
            blocks = [r[:, part] if r.shape[1] == rows * pixels else r[...] for r in ins]
            made = made_of(blocks, spread).astype(bf16)
            kept[:, part] = made
            for m in range(count):
                value = jnp.dot(w[m], made, preferred_element_type=f32).astype(bf16)
                if not splits:
                    outs[0][places[0] ^ q, m] = value
                else:
                    side, place = m // half, m % half
                    bit = splits[side]
                    kind = 1 if q & bit else 0
                    outs[2 * side + kind][queue[side].index(q & ~bit), place] = value

    queue = [sorted({q & ~bit for q in range(rows)}) for bit in splits or []]
    if not splits:
        outs = [shape_of((rows, count, chans, pixels), bf16)]
    else:
        outs = [shape_of((rows // 2, half, chans, pixels), bf16)] * 4
    got = call(
        body, [shape_of((units, rows * pixels), bf16)] + outs, places, *operands, turned
    )
    return got[0], got[1:]


def grads_kernel(places, left, pieces, dims, count, chans):
    rows, batch, pixels = dims
    units = left.shape[0]
    share = units // 2
    order = sum(col_order(count), [])

    def body(places, left, *refs):
        xs = refs[: len(pieces)]
        mine, other = refs[len(pieces) :]
        for place, m in enumerate(order):
            x = jnp.concatenate([piece_of(xs, places, rows, q, place) for q in range(rows)], axis=1)
            value = lax.dot_general(x, left[...], last_last, preferred_element_type=f32).astype(bf16)
            mine[places[1] ^ m] = value[:, :share]
            other[places[1] ^ m] = value[:, share:]

    return call(body, [shape_of((count, chans, share), bf16)] * 2, places, left, *pieces)


def add_kernel(places, mine, got):
    def body(places, mine, got, out):
        for j in range(mine.shape[0]):
            out[j] = (mine[j].astype(f32) + got[j].astype(f32)).astype(bf16)

    return call(body, [shape_of(mine.shape, bf16)], places, mine, got)[0]


def finish_kernel(places, pieces, scale):
    count, chans, share = pieces.shape

    def body(places, pieces, out):
        wide = jnp.concatenate([pieces[j].astype(f32) for j in range(count)], axis=1)
        out[...] = wide * scale

    return call(body, [shape_of((chans, count * share), f32)], places, pieces)[0]


def own_units(vector):
    count = lax.axis_size("col")
    span = vector.shape[0] // 2
    share = span // count
    me = lax.axis_index("col")
    side = lax.axis_index("dp")
    mine = lax.dynamic_slice_in_dim(vector, side * span + me * share, share)
    other = lax.dynamic_slice_in_dim(vector, (1 - side) * span + me * share, share)
    return jnp.concatenate([mine, other])


def add_over(value, axis):
    n = lax.axis_size(axis)
    step = 1
    while step < n:
        value = value + swap(value, axis, step)
        step *= 2
    return value


def exchange_rows(low, high):
    count = lax.axis_size("row")
    forward = [(i, i + 1) for i in range(count - 1)]
    backward = [(i + 1, i) for i in range(count - 1)]
    return lax.ppermute(low, "row", forward), lax.ppermute(high, "row", backward)


EDGE = 8


def fill_padded(padded, low, mid, high):
    reach, height, width = low.shape[0], mid.shape[0], mid.shape[2]
    zeros = jnp.zeros(padded.shape[:2] + (EDGE, padded.shape[3]), f32)
    padded[:, :, :EDGE, :] = zeros
    padded[:, :, EDGE + width :, :] = zeros
    padded[:reach, :, EDGE : EDGE + width, :] = low[...].astype(f32)
    padded[reach : reach + height, :, EDGE : EDGE + width, :] = mid[...].astype(f32)
    padded[reach + height :, :, EDGE : EDGE + width, :] = high[...].astype(f32)


def lane_chunks(chans):
    return [slice(c, min(c + 128, chans)) for c in range(0, chans, 128)]


def depthwise(places, low, mid, high, kernel, extra, flip):
    height, batch, width, chans = mid.shape
    span = kernel.shape[0]
    reach = span // 2

    def body(places, low, mid, high, kern, *refs):
        out, padded = refs[-2:]
        fill_padded(padded, low, mid, high)

        @pl.loop(0, batch)
        def _(b):
            for lanes in lane_chunks(chans):
                sums = [None] * height
                for r in range(height + 2 * reach):
                    for j in range(span):
                        start = EDGE + j - reach
                        window = padded[r, b, start : start + width, lanes]
                        for h in range(max(0, r - span + 1), min(height, r + 1)):
                            i = r - h
                            tap = (span - 1 - i, span - 1 - j) if flip else (i, j)
                            term = kern[tap[0], tap[1] : tap[1] + 1, lanes] * window
                            sums[h] = term if sums[h] is None else sums[h] + term
                for h in range(height):
                    value = sums[h]
                    if extra is not None:
                        value = value + refs[0][h, b, :, lanes].astype(f32)
                    out[h, b, :, lanes] = value.astype(out.dtype)

    more = [] if extra is None else [extra]
    operands = [low, mid, high, kernel] + more
    return pl.pallas_call(
        body,
        out_shape=shape_of(mid.shape, f32 if extra is None else bf16),
        in_specs=[in_smem] + [in_vmem] * len(operands),
        out_specs=in_vmem,
        scratch_shapes=[pltpu.VMEM((height + 2 * reach, batch, width + 2 * EDGE, chans), f32)],
        compiler_params=pltpu.CompilerParams(vmem_limit_bytes=VMEM_BYTES),
        cost_estimate=pl.CostEstimate(flops=0, bytes_accessed=0, transcendentals=0),
    )(places, *operands)


def kernel_terms(places, low, mid, high, grad, span):
    height, batch, width, chans = mid.shape
    reach = span // 2

    def body(places, low, mid, high, grad, out, padded, sums):
        fill_padded(padded, low, mid, high)
        for lanes in lane_chunks(chans):
            for i in range(span):

                def step(b, total):
                    total = list(total)
                    for h in range(height):
                        piece = grad[h, b, :, lanes]
                        for j in range(span):
                            start = EDGE + j - reach
                            both = piece * padded[h + i, b, start : start + width, lanes]
                            total[j] = total[j] + jnp.sum(both.reshape(-1, 8, both.shape[1]), axis=0)
                    return tuple(total)

                zero = jnp.zeros((8, lanes.stop - lanes.start), f32)
                total = lax.fori_loop(0, batch, step, (zero,) * span)
                for j in range(span):
                    sums[i, j, :, lanes] = total[j]
        for i in range(span):
            out[i] = jnp.sum(sums[i], axis=1)

    operands = [low, mid, high, grad]
    return pl.pallas_call(
        body,
        out_shape=shape_of((span, span, chans), f32),
        in_specs=[in_smem] + [in_vmem] * len(operands),
        out_specs=in_vmem,
        scratch_shapes=[
            pltpu.VMEM((height + 2 * reach, batch, width + 2 * EDGE, chans), f32),
            pltpu.VMEM((span, span, 8, chans), f32),
        ],
        compiler_params=pltpu.CompilerParams(vmem_limit_bytes=VMEM_BYTES),
        cost_estimate=pl.CostEstimate(flops=0, bytes_accessed=0, transcendentals=0),
    )(places, *operands)


def local(images, cotangent, kernel, w_in, b_in, grn_gamma, grn_beta, w_out):
    height, batch, width, chans = images.shape
    span = kernel.shape[0]
    reach = span // 2
    col_count = lax.axis_size("col")
    row_count = lax.axis_size("row")
    all_chans = chans * col_count
    all_units = b_in.shape[0] * row_count
    pixels = height * batch * width
    group_pix = pixels * row_count
    scale_grad = 1.0 / math.sqrt(group_pix * lax.axis_size("dp"))

    places = jnp.stack([lax.axis_index("row"), lax.axis_index("col")]).astype(jnp.int32)
    dims = (row_count, batch, pixels)

    def turned(tile):
        return tile.transpose(3, 1, 0, 2).reshape(chans, pixels)

    def natural(block):
        return block.reshape(chans, batch, height, width).transpose(2, 1, 3, 0)


    pieces, cot_turned, low, high = prepare(places, images, cotangent, w_in, reach)
    cot_hops = first_hops(cot_turned, True)
    low, high = exchange_rows(low, high)
    bias, gamma, beta = own_units(b_in), own_units(grn_gamma), own_units(grn_beta)

    conv_out = depthwise(places, low, images, high, kernel, None, False)
    mean_own = jnp.mean(conv_out, axis=-1)
    dev_own = conv_out - mean_own[..., None]
    stats = jnp.stack([mean_own, jnp.sum(dev_own * dev_own, axis=-1)])
    stats = after(stats, cot_hops)
    cot_all = gather_rows(stack_cols(gather_cols(cot_turned, cot_hops)))
    stats = [stats] + [swap(stats, "col", m) for m in range(1, col_count)]
    mean_pix = sum(s[0] for s in stats) / col_count
    var_pix = sum(s[1] + chans * (s[0] - mean_pix) ** 2 for s in stats) / all_chans
    inv_std = lax.rsqrt(var_pix + epsilon)[..., None]
    standard = (conv_out - mean_pix[..., None]) * inv_std
    bits = row_bits()
    normed = turned(standard.astype(bf16))
    normed_cols = gather_cols(normed, first_hops(normed))
    normed_stack = after(stack_cols(normed_cols), cot_all[1], cot_all[2])
    normed_all = gather_rows(normed_stack)
    w_in_there = lax.all_to_all(after(pieces, normed_stack), "col", 0, 0)
    w_in_there = after(w_in_there, normed_all[1], normed_all[2], cot_all[3], cot_all[4])
    w_in_all, w_in_turned = join_weights(places, w_in_there, swap(w_in_there, "dp", 1))
    pieces = after(prepare_out(places, w_out.T), w_in_there)
    w_out_there = lax.all_to_all(pieces, "col", 0, 0)
    act, slope, square = hidden_kernel(places, normed_all, w_in_all, bias, dims)
    norm_chan = jnp.sqrt(square + epsilon)
    norm_rows = add_over(jnp.sum(norm_chan, axis=0), "row")
    w_out_there = after(w_out_there, norm_rows)
    w_out_all, w_out_turned = join_weights(places, w_out_there, swap(w_out_there, "dp", 1))
    norm_sum = add_over(norm_rows, "col")
    denom = norm_sum / all_units + epsilon
    gamma, beta = gamma[:, None], beta[:, None]
    gain = gamma * (norm_chan / denom) + 1.0
    grad_gated, pull = back_kernel(places, cot_all, w_out_all, act, dims)
    share_back = gamma * pull / denom / norm_chan

    grad_pre, grad_parts = project_kernel(
        places,
        lambda b, spread: (b[0] * spread(b[3]) + b[1] * spread(b[4])) * b[2],
        [grad_gated, act, slope, gain, share_back],
        w_in_turned,
        dims,
        (bits[0], bits[-1]),
    )
    gated = gated_kernel(places, after(act, grad_parts), gain, beta, dims)
    w_out_mine, w_out_other = grads_kernel(places, gated, cot_all, dims, col_count, chans)
    w_out_sums = add_kernel(places, w_out_mine, swap(w_out_other, "dp", 1))
    w_out_back = lax.all_to_all(after(w_out_sums, w_out_there), "col", 0, 0)
    w_out_grad = finish_kernel(places, w_out_back, scale_grad).T
    _, out_parts = project_kernel(
        places, lambda b, spread: b[0], [gated], w_out_turned, dims, (bits[0], bits[-1])
    )
    w_in_mine, w_in_other = grads_kernel(
        places, grad_pre, normed_all, dims, col_count, chans
    )
    w_in_sums = add_kernel(places, w_in_mine, swap(w_in_other, "dp", 1))

    near_a, far_a, near_b, far_b = grad_parts
    shade = (w_out_other, w_in_other, out_parts[0])
    even = halve_sum(near_a, far_a, "row", bits, shade)
    odd = halve_sum(near_b, far_b, "row", bits[::-1], shade)
    down = [1 << i for i in range((col_count - 1).bit_length())]
    near_a, far_a, near_b, far_b = out_parts
    far_a, far_b = after((far_a, far_b), even, odd)
    out_even = halve_sum(near_a, far_a, "row", bits)
    out_odd = halve_sum(near_b, far_b, "row", bits[::-1])
    odd = after(odd, w_out_back)
    grad_normed = natural(pin(halve_sum(even, odd, "col", down)))

    sums = jnp.stack([jnp.sum(grad_normed, axis=-1), jnp.sum(grad_normed * standard, axis=-1)])
    sums = sum([swap(sums, "col", m) for m in range(1, col_count)], sums) / all_chans
    out_odd = after(out_odd, sums)
    w_in_back = lax.all_to_all(after(w_in_sums, sums), "col", 0, 0)
    w_in_grad = finish_kernel(places, w_in_back, scale_grad)
    grad_conv = inv_std * (grad_normed - sums[0][..., None] - standard * sums[1][..., None])
    edge = grad_conv.astype(bf16)
    low_grad, high_grad = exchange_rows(edge[height - reach :], edge[:reach])
    x_grad = depthwise(places, low_grad, grad_conv, high_grad, kernel, cotangent, True)
    kern = kernel_terms(places, low, images, high, after(grad_conv, low_grad, high_grad), span)
    steps = [("dp", 1)] + [("row", 1 << i) for i in range((row_count - 1).bit_length())]
    for axis, step in steps:
        kern = kern.astype(bf16)
        kern = kern.astype(f32) + swap(kern, axis, step).astype(f32)
    kernel_grad = kern * scale_grad
    branch = halve_sum(out_even, out_odd, "col", down, (x_grad,))
    branch = natural(pin(branch))
    result = (images.astype(f32) + branch.astype(f32)).astype(bf16)
    return (result, x_grad, w_in_grad, w_out_grad, kernel_grad)


def solution(mesh):
    return jax.shard_map(
        local,
        mesh=mesh,
        in_specs=(
            P("row", "dp", None, "col"),
            P("row", "dp", None, "col"),
            P(None, None, "col"),
            P("col", ("row", "dp")),
            P("row"),
            P("row"),
            P("row"),
            P(("row", "dp"), "col"),
        ),
        out_specs=(
            P("row", "dp", None, "col"),
            P("row", "dp", None, "col"),
            P("col", ("row", "dp")),
            P(("row", "dp"), "col"),
            P(None, None, "col"),
        ),
        check_vma=False,
    )
```
